32 devices in a mesh: pipe: 4 (over z), seq: 4 (over y, x), tp: 2 (over core).
Axes of the slice: x: 2, y: 2, z: 4, core: 2. Of those that a mesh axis runs over, the one named last changes fastest.
Arguments:
- layer_inputs: bfloat16 [4, 512, 4096], P('pipe', ('seq', 'tp')), may hold values from -6 to 6
- out_grad: bfloat16 [512, 4096], P('seq', 'tp'), may hold values from -6 to 6
- short_weights: bfloat16 [4, 7, 3, 4096], P('pipe', None, None, 'tp'), may hold values from -2 to 2
- long_filters: bfloat16 [4, 256, 128], P('pipe', 'tp'), may hold values from -0.15625 to 0.15625
- out_weights: bfloat16 [4, 4096, 4096], P('pipe', 'tp', 'seq'), may hold values from -0.09375 to 0.09375
Outputs:
- input_grad: bfloat16 [4, 512, 4096], P('pipe', 'seq', 'tp')
- short_grad: float32 [4, 7, 3, 4096], P('pipe', None, None, 'tp')
- long_grad: float32 [4, 256, 128], P('pipe', 'tp')
The draws below stay inside these ranges and needn't reach their ends.
All inputs are finite; a program needn't handle non-finite values.
Results may differ from the reference program's by a relative error of at most 0.03.
Values may be sent and summed in bfloat16 or wider, within the bound.
A program may use at most 192 MiB of HBM per device.

```python
import jax
import jax.numpy as jnp
from jax import lax

D = 4096
KL = 128
KS = 7
SECTIONS = 4
TOKENS = 512
GROUPS = 256


def levels(key, shape, pieces, least, top_value):
    loudness = 1.0
    for dim, parts in pieces:
        heights = jax.random.uniform(jax.random.fold_in(jax.random.fold_in(key, 6), dim), (parts,), jnp.float32, least / len(pieces), top_value / len(pieces))
        loudness = loudness * jnp.repeat(jnp.exp(heights), shape[dim] // parts).reshape((-1,) + (1,) * (len(shape) - 1 - dim))
    return loudness


def scatter_about(stream_key, shape, scale, limit, cuts=(), kind=jnp.bfloat16):
    drawn = scale * jax.random.normal(stream_key, shape, jnp.float32)
    if cuts:
        drawn = drawn * levels(stream_key, shape, cuts, -0.22, 0.18)
    return jnp.clip(drawn, -limit, limit).astype(kind)


def setup_inputs(seed: int = 0) -> dict:
    splits = jax.random.split(jax.random.key(seed), 6)
    return {
        "layer_inputs": scatter_about(splits[0], (SECTIONS, TOKENS, D), 1.0, 6.0, ((0, 4), (1, 8))),
        "out_grad": scatter_about(splits[1], (TOKENS, D), 1.0, 6.0, ((0, 4), (1, 2))),
        "short_weights": scatter_about(splits[2], (SECTIONS, KS, 3, D), KS ** -0.5, 2.0, ((0, 4), (3, 2))),
        "long_filters": scatter_about(splits[3], (SECTIONS, GROUPS, KL), (11 * KL) ** -0.5, 0.15625, ((0, 4), (1, 2))),
        "out_weights": scatter_about(splits[4], (SECTIONS, D, D), D ** -0.5, 0.09375, ((0, 4), (1, 2), (2, 4))),
    }


exact_mode = lax.Precision.HIGHEST


def toeplitz_blocks(filters):
    groups, kernel_width = filters.shape
    base_row = jnp.concatenate([jnp.zeros((groups, 1), filters.dtype), filters[:, ::-1], jnp.zeros((groups, kernel_width), filters.dtype)], axis=1)
    tiled = jnp.tile(base_row, (1, kernel_width))[:, : 2 * kernel_width * kernel_width]
    return tiled.reshape(groups, kernel_width, 2 * kernel_width)


def lag_sums(products):
    groups, kernel_width, window = products.shape
    flattened = products.reshape(groups, kernel_width * window)
    flattened = jnp.pad(flattened, ((0, 0), (0, kernel_width)))
    skewed = flattened.reshape(groups, kernel_width, window + 1)
    totals = jnp.sum(skewed, axis=1)
    return totals[:, 1: kernel_width + 1][:, ::-1]


def featurize(source, weights):
    tap_count = weights.shape[0]
    row_count = source.shape[0] - tap_count + 1
    running = jnp.zeros((weights.shape[1], row_count, source.shape[1]), jnp.float32)
    for offset in range(tap_count):
        start = tap_count - 1 - offset
        running = running + weights[offset][:, None, :] * source[start: start + row_count][None]
    return running


def spread_back(feature_grads, weights):
    tap_count = weights.shape[0]
    row_count = feature_grads.shape[1] - tap_count + 1
    running = jnp.zeros((row_count, feature_grads.shape[2]), jnp.float32)
    for offset in range(tap_count):
        running = running + jnp.sum(weights[offset][:, None, :] * feature_grads[:, offset: offset + row_count], axis=0)
    return running


def weight_grads(feature_grads, source):
    row_count = feature_grads.shape[1]
    tap_count = source.shape[0] - row_count + 1
    terms = []
    for offset in range(tap_count):
        start = tap_count - 1 - offset
        terms.append(jnp.sum(feature_grads * source[start: start + row_count][None], axis=1))
    return jnp.stack(terms)


def long_forward(padded, toeplitz, groups):
    kernel_width = toeplitz.shape[1]
    blocks = padded.astype(jnp.float32).reshape(padded.shape[0] // kernel_width, kernel_width, groups, -1)
    matrix = toeplitz.astype(jnp.float32)
    earlier = jnp.einsum("gij,bjgc->bigc", matrix[:, :, :kernel_width], blocks[:-1], precision=exact_mode)
    current = jnp.einsum("gij,bjgc->bigc", matrix[:, :, kernel_width:], blocks[1:], precision=exact_mode)
    return (earlier + current).reshape(-1, padded.shape[1])


def long_backward(padded, toeplitz, groups):
    kernel_width = toeplitz.shape[1]
    blocks = padded.astype(jnp.float32).reshape(padded.shape[0] // kernel_width, kernel_width, groups, -1)
    matrix = toeplitz.astype(jnp.float32)
    current = jnp.einsum("gij,bigc->bjgc", matrix[:, :, kernel_width:], blocks[:-1], precision=exact_mode)
    following = jnp.einsum("gij,bigc->bjgc", matrix[:, :, :kernel_width], blocks[1:], precision=exact_mode)
    return (current + following).reshape(-1, padded.shape[1])


def filter_grads(mixed_grad, padded, groups):
    kernel_width = padded.shape[0] - mixed_grad.shape[0]
    grad_blocks = mixed_grad.astype(jnp.float32).reshape(-1, kernel_width, groups, mixed_grad.shape[1] // groups)
    value_blocks = padded.astype(jnp.float32).reshape(-1, kernel_width, groups, mixed_grad.shape[1] // groups)
    earlier = jnp.einsum("bigc,bjgc->gij", grad_blocks, value_blocks[:-1], precision=exact_mode)
    current = jnp.einsum("bigc,bjgc->gij", grad_blocks, value_blocks[1:], precision=exact_mode)
    return lag_sums(jnp.concatenate([earlier, current], axis=2))


def section_grads(layer_input, incoming, short_weights, filters, out_weight):
    tap_count = short_weights.shape[0]
    groups, kernel_width = filters.shape
    channels = layer_input.shape[1]
    weights = short_weights.astype(jnp.float32)
    source = jnp.concatenate([jnp.zeros((tap_count - 1, channels), jnp.float32), layer_input.astype(jnp.float32)], axis=0)
    features = featurize(source, weights)
    products = (features[1] * features[2]).astype(jnp.bfloat16)
    padded = jnp.concatenate([jnp.zeros((kernel_width, channels), jnp.bfloat16), products], axis=0)
    toeplitz = toeplitz_blocks(filters)
    mixed_rows = long_forward(padded, toeplitz, groups)
    gradient = incoming.astype(jnp.float32)
    dense_part = jnp.dot(incoming, jnp.transpose(out_weight), preferred_element_type=jnp.float32).astype(jnp.bfloat16)
    dense_float = dense_part.astype(jnp.float32)
    query_grad = dense_float * mixed_rows
    mixed_grad = (dense_float * features[0]).astype(jnp.bfloat16)
    trailing_grad = jnp.concatenate([mixed_grad, jnp.zeros((kernel_width, channels), jnp.bfloat16)], axis=0)
    product_grad = long_backward(trailing_grad, toeplitz, groups)
    feature_grads = jnp.stack([query_grad, product_grad * features[2], product_grad * features[1]])
    extended = jnp.concatenate([feature_grads, jnp.zeros((3, tap_count - 1, channels), jnp.float32)], axis=1)
    input_grad = (gradient + spread_back(extended, weights)).astype(jnp.bfloat16)
    return input_grad, weight_grads(feature_grads, source), filter_grads(mixed_grad, padded, groups)


def reference(layer_inputs, out_grad, short_weights, long_filters, out_weights):
    sections = layer_inputs.shape[0]
    incoming = out_grad
    input_list = []
    short_list = []
    long_list = []
    for section_index in range(sections - 1, -1, -1):
        input_grad, short_grad, long_grad = section_grads(layer_inputs[section_index], incoming, short_weights[section_index], long_filters[section_index], out_weights[section_index])
        input_list.append(input_grad)
        short_list.append(short_grad)
        long_list.append(long_grad)
        incoming = input_grad
    return jnp.stack(input_list[::-1]), jnp.stack(short_list[::-1]), jnp.stack(long_list[::-1])
```

```python
import functools

import jax
import jax.numpy as jnp
from jax import lax
from jax.experimental import pallas as pl
from jax.experimental.pallas import tpu as pltpu
from jax.sharding import PartitionSpec as P

MESH = pl.DeviceIdType.MESH
F32 = jnp.float32
BF16 = jnp.bfloat16
TAP_ROWS = 32


def remote(src, dst, send_sem, recv_sem, device):
    return pltpu.make_async_remote_copy(
        src_ref=src,
        dst_ref=dst,
        send_sem=send_sem,
        recv_sem=recv_sem,
        device_id=device,
        device_id_type=MESH,
    )


def aligned(index, size):
    return pl.ds(pl.multiple_of(index * size, size), size)


def kernel(
    dims,
    x_hbm,
    og_hbm,
    taps_hbm,
    filt_hbm,
    w_hbm,
    ig_out,
    short_out,
    long_out,
    xin,
    gin,
    taps_in,
    filt,
    w_vmem,
    xt,
    cols,
    feats,
    mixed,
    dkv,
    kv,
    dm,
    toep,
    gbuf,
    part,
    rs,
    ig,
    ot,
    short_cols,
    short_rows,
    long_rows,
    x_send,
    x_recv,
    og_send,
    og_recv,
    small_send,
    small_recv,
    sib_send,
    sib_recv,
    z_send,
    z_recv,
    rs_send,
    rs_recv,
    ig_send,
    ig_recv,
    sg_send,
    sg_recv,
    lg_send,
    lg_recv,
    local_sem,
):
    sections, n, ntp, tokens, cb, groups, width, taps, chunk = dims
    m = n * ntp
    chunks = cb // chunk
    blocks = tokens // width
    gw = cb // groups
    tl = tokens // n
    p, q, c = lax.axis_index("pipe"), lax.axis_index("seq"), lax.axis_index("tp")
    b = q * ntp + c
    half, slot = b // n, lax.rem(b, n)
    sibling = (p, q, 1 - c)
    owns = c == half
    last = p == sections - 1
    mine = aligned(c, cb)
    theirs = aligned(1 - c, cb)

    def place(block):
        return (p, block // ntp, lax.rem(block, ntp))

    barrier = pltpu.get_barrier_semaphore()
    for r in range(1, m):
        pl.semaphore_signal(
            barrier, inc=1, device_id=place(lax.rem(b + r, m)), device_id_type=MESH
        )

    @pl.when(p > 0)
    def _():
        pl.semaphore_signal(barrier, inc=1, device_id=(p - 1, q, c), device_id_type=MESH)

    @pl.when(p < sections - 1)
    def _():
        pl.semaphore_signal(barrier, inc=1, device_id=(p + 1, q, c), device_id_type=MESH)

    w_copy = pltpu.make_async_copy(w_hbm, w_vmem, local_sem.at[0])
    w_copy.start()
    x_rows = tokens // m
    x_local = pltpu.make_async_copy(
        x_hbm.at[:, aligned(b, cb)], xin.at[aligned(b, x_rows)], local_sem.at[1]
    )
    x_local.start()
    ends = (p > 0).astype(jnp.int32) + (p < sections - 1).astype(jnp.int32)
    pl.semaphore_wait(barrier, m - 1 + ends)

    def og_copy(j):
        block = c * n + j
        return block, remote(
            og_hbm.at[:, aligned(j, cb)],
            gin.at[aligned(q, tl)],
            og_send.at[j],
            og_recv.at[q],
            place(block),
        )

    @pl.when(last)
    def _():
        for j in range(n):
            block, copy = og_copy(j)

            @pl.when(block != b)
            def _():
                copy.start()

        @pl.when(owns)
        def _():
            own = pltpu.make_async_copy(
                og_hbm.at[:, aligned(slot, cb)], gin.at[aligned(q, tl)], local_sem.at[2]
            )
            own.start()
            own.wait()

    def x_copy(r):
        block = lax.rem(b + r, m)
        return remote(
            x_hbm.at[:, aligned(block, cb)],
            xin.at[aligned(b, x_rows)],
            x_send.at[r],
            x_recv.at[r],
            place(block),
        )

    for r in range(1, m):
        x_copy(r).start()

    other = lax.rem(q * ntp + 1 - c, n)
    taps_copy = remote(
        taps_hbm.at[:, aligned(other, cb)], taps_in, small_send.at[0], small_recv.at[0], sibling
    )
    filt_copy = remote(
        filt_hbm.at[aligned(other, groups)], filt, small_send.at[1], small_recv.at[1], sibling
    )

    @pl.when(owns)
    def _():
        taps_copy.start()
        filt_copy.start()
        taps_own = pltpu.make_async_copy(
            taps_hbm.at[:, aligned(slot, cb)], taps_in, local_sem.at[3]
        )
        filt_own = pltpu.make_async_copy(filt_hbm.at[aligned(slot, groups)], filt, local_sem.at[4])
        taps_own.start()
        filt_own.start()
        taps_own.wait()
        filt_own.wait()

    def sib_copy(k):
        rows = pl.ds(pl.multiple_of(c * cb + k * chunk, chunk), chunk)
        return remote(gbuf.at[rows], gbuf.at[rows], sib_send.at[k], sib_recv.at[k], sibling)

    def sib_wait(k):
        rows = pl.ds(pl.multiple_of((1 - c) * cb + k * chunk, chunk), chunk)
        remote(
            gbuf.at[rows], gbuf.at[rows], sib_send.at[k], sib_recv.at[k], sibling
        ).wait_recv()

    def part_copy(j, k):
        block = c * n + j
        rows = pl.ds(k * chunk, chunk)
        return block, remote(
            part.at[j, rows],
            rs.at[q, rows],
            rs_send.at[k, j],
            rs_recv.at[k, q],
            place(block),
        )

    def dense():
        for k in range(chunks):
            sib_wait(k)
        for k in range(chunks):
            rows = pl.ds(k * chunk, chunk)

            def one(step, carry):
                j = lax.rem(step + slot + 1, n)
                block, copy = part_copy(j, k)
                w_rows = pl.ds(pl.multiple_of(j * cb + k * chunk, chunk), chunk)
                product = jnp.dot(
                    w_vmem[w_rows, :], gbuf[...], preferred_element_type=F32
                ).astype(BF16)

                @pl.when(block != b)
                def _():
                    part[j, rows, :] = product
                    copy.start()

                @pl.when(block == b)
                def _():
                    rs[q, rows, :] = product

                return carry

            lax.fori_loop(0, n, one, 0)

    @pl.when(last)
    def _():
        for source in range(n):

            @pl.when(jnp.logical_or(source != q, jnp.logical_not(owns)))
            def _():
                remote(
                    og_hbm.at[:, pl.ds(0, cb)],
                    gin.at[pl.ds(source * tl, tl)],
                    og_send.at[0],
                    og_recv.at[source],
                    sibling,
                ).wait_recv()

        for k in range(chunks):
            gbuf[pl.ds(pl.multiple_of(c * cb + k * chunk, chunk), chunk), :] = (
                gin[:, pl.ds(k * chunk, chunk)].astype(F32).T.astype(BF16)
            )
            sib_copy(k).start()
        w_copy.wait()
        dense()

    x_local.wait()
    for r in range(1, m):
        source = lax.rem(b - r + m, m)
        remote(
            x_hbm.at[:, pl.ds(0, cb)],
            xin.at[aligned(source, x_rows)],
            x_send.at[r],
            x_recv.at[r],
            sibling,
        ).wait_recv()
    for k in range(chunks):
        span = pl.ds(k * chunk, chunk)
        xt[span, :] = xin[:, span].astype(F32).T

    @pl.when(jnp.logical_not(owns))
    def _():
        taps_copy.wait_recv()
        filt_copy.wait_recv()

    cols[...] = taps_in[...].T
    lane = lax.broadcasted_iota(jnp.int32, (gw, tokens), 1)

    def later(value, by):
        if by == 0:
            return value
        return jnp.where(lane >= by, pltpu.roll(value, by, 1), 0.0)

    def stacked(value):
        return jnp.concatenate(
            [value[:, i * width : (i + 1) * width] for i in range(blocks)], axis=0
        )

    def windows(value):
        wide = jnp.concatenate([value, jnp.zeros((gw, width), value.dtype)], axis=1)
        return jnp.concatenate(
            [wide[:, i * width : (i + 2) * width] for i in range(blocks)], axis=0
        )

    def group_rows(g):
        return aligned(g, gw)

    def recompute(g, carry):
        rows = group_rows(g)
        source = xt[rows, :]
        weight = cols[rows, :]
        running = [jnp.zeros((gw, tokens), F32)] * 3
        for j in range(taps):
            shifted = later(source, j)
            for f in range(3):
                running[f] = running[f] + weight[:, 3 * j + f : 3 * j + f + 1] * shifted
        for f in range(3):
            feats[f, rows, :] = running[f]
        product = (running[1] * running[2]).astype(BF16)
        kv[rows, :] = product
        tap_row = jnp.concatenate([filt[pl.ds(g, 1), :], jnp.zeros((1, width), F32)], axis=1)
        band = pltpu.roll(
            jnp.broadcast_to(tap_row, (width, 2 * width)), 0, 1, stride=1, stride_axis=0
        ).astype(BF16)
        toep[g] = band
        spread = jnp.dot(stacked(product), band, preferred_element_type=F32)
        for i in range(blocks):
            value = spread[i * gw : (i + 1) * gw, :width]
            if i > 0:
                value = value + spread[(i - 1) * gw : i * gw, width:]
            mixed[rows, pl.ds(i * width, width)] = value
        return carry

    lax.fori_loop(0, groups, recompute, 0)

    def z_copy(k):
        rows = pl.ds(pl.multiple_of(c * cb + k * chunk, chunk), chunk)
        return remote(
            ig.at[pl.ds(k * chunk, chunk)],
            gbuf.at[rows],
            z_send.at[k],
            z_recv.at[k],
            (jnp.maximum(p - 1, 0), q, c),
        )

    @pl.when(jnp.logical_not(last))
    def _():
        for k in range(chunks):
            z_copy(k).wait_recv()
            sib_copy(k).start()
        w_copy.wait()
        dense()

    def backward(g, carry):
        rows = group_rows(g)
        gate = rs[0, rows, :].astype(F32)
        for source in range(1, n):
            gate = gate + rs[source, rows, :].astype(F32)
        gate = gate.astype(BF16).astype(F32)
        mixed_grad = (gate * feats[0, rows, :]).astype(BF16)
        dm[rows, :] = mixed_grad
        result = lax.dot_general(
            windows(mixed_grad), toep[g], (((1,), (1,)), ((), ())), preferred_element_type=F32
        )
        product_grad = jnp.concatenate(
            [result[i * gw : (i + 1) * gw] for i in range(blocks)], axis=1
        )
        dkv[rows, :] = product_grad
        query_grad = gate * mixed[rows, :]
        mixed[rows, :] = query_grad
        grads = (query_grad, product_grad * feats[2, rows, :], product_grad * feats[1, rows, :])
        weight = cols[rows, :]
        total = None
        for j in range(taps - 1, -1, -1):
            term = weight[:, 3 * j : 3 * j + 1] * grads[0]
            for f in (1, 2):
                term = term + weight[:, 3 * j + f : 3 * j + f + 1] * grads[f]
            if total is None:
                total = term
            else:
                moved = jnp.where(lane < tokens - 1, pltpu.roll(total, tokens - 1, 1), 0.0)
                total = moved + term
        g_rows = pl.ds(pl.multiple_of(c * cb + g * gw, gw), gw)
        ig[rows, :] = (gbuf[g_rows, :].astype(F32) + total).astype(BF16)
        return carry

    per_chunk = chunk // gw
    for k in range(chunks):
        for source in range(n):

            @pl.when(jnp.logical_or(source != q, jnp.logical_not(owns)))
            def _():
                rows = pl.ds(k * chunk, chunk)
                remote(
                    part.at[0, rows],
                    rs.at[source, rows],
                    rs_send.at[k, 0],
                    rs_recv.at[k, source],
                    sibling,
                ).wait_recv()

        lax.fori_loop(k * per_chunk, (k + 1) * per_chunk, backward, 0)

        @pl.when(p > 0)
        def _():
            z_copy(k).start()

    for k in range(chunks):
        span = pl.ds(k * chunk, chunk)
        ot[:, span] = ig[span, :].astype(F32).T.astype(BF16)

    def give(src, dst, send_sem, recv_sem, target, own_sem):
        copy = remote(src, dst, send_sem.at[target], recv_sem.at[slot], (p, target, half))

        def start():
            @pl.when(jnp.logical_or(target != q, jnp.logical_not(owns)))
            def _():
                copy.start()

            @pl.when(jnp.logical_and(target == q, owns))
            def _():
                own = pltpu.make_async_copy(src, dst, own_sem)
                own.start()
                own.wait()

        def sent():
            @pl.when(jnp.logical_or(target != q, jnp.logical_not(owns)))
            def _():
                copy.wait_send()

        return start, sent

    def ig_give(target):
        return give(
            ot.at[pl.ds(target * tl, tl)],
            ig_out.at[:, aligned(slot, cb)],
            ig_send,
            ig_recv,
            target,
            local_sem.at[5],
        )

    def short_give(target):
        return give(
            short_rows, short_out.at[:, aligned(slot, cb)], sg_send, sg_recv, target, local_sem.at[6]
        )

    def long_give(target):
        return give(
            long_rows, long_out.at[aligned(slot, groups)], lg_send, lg_recv, target, local_sem.at[7]
        )

    for target in range(n):
        ig_give(target)[0]()

    column = lax.broadcasted_iota(jnp.int32, (gw, TAP_ROWS), 1)
    low = lax.broadcasted_iota(jnp.int32, (8, 2 * width), 0)

    def filters(g, carry):
        rows = group_rows(g)
        source = xt[rows, :]
        product_grad = dkv[rows, :]
        grads = (
            mixed[rows, :],
            product_grad * feats[2, rows, :],
            product_grad * feats[1, rows, :],
        )
        sums = jnp.zeros((gw, TAP_ROWS), F32)
        for j in range(taps):
            shifted = later(source, j)
            for f in range(3):
                total = jnp.sum(grads[f] * shifted, axis=1, keepdims=True)
                sums = jnp.where(column == 3 * j + f, total, sums)
        short_cols[rows, :] = sums
        lags = lax.dot_general(
            stacked(kv[rows, :]),
            windows(dm[rows, :]),
            (((0,), (0,)), ((), ())),
            preferred_element_type=F32,
        )
        size = width
        while size > 8:
            size //= 2
            lags = lags[:size] + pltpu.roll(lags[size:], 2 * width - size, 1)
        for bit in (4, 2, 1):
            lags = jnp.where((low & bit) != 0, pltpu.roll(lags, 2 * width - bit, 1), lags)
        long_rows[pl.ds(g, 1), :] = jnp.sum(lags, axis=0, keepdims=True)[:, :width]
        return carry

    lax.fori_loop(0, groups, filters, 0)
    short_rows[...] = short_cols[...].T
    for target in range(n):
        short_give(target)[0]()
        long_give(target)[0]()

    for j in range(n):

        @pl.when(c * n + j != b)
        def _():
            for src, dst, send, recv in (
                (ot.at[pl.ds(0, tl)], ig_out.at[:, pl.ds(j * cb, cb)], ig_send, ig_recv),
                (short_rows, short_out.at[:, pl.ds(j * cb, cb)], sg_send, sg_recv),
                (long_rows, long_out.at[pl.ds(j * groups, groups)], lg_send, lg_recv),
            ):
                remote(src, dst, send.at[0], recv.at[j], sibling).wait_recv()
            for k in range(chunks):
                part_copy(j, k)[1].wait_send()

            @pl.when(last)
            def _():
                og_copy(j)[1].wait_send()

    for target in range(n):
        ig_give(target)[1]()
        short_give(target)[1]()
        long_give(target)[1]()
    for r in range(1, m):
        x_copy(r).wait_send()

    @pl.when(owns)
    def _():
        taps_copy.wait_send()
        filt_copy.wait_send()

    for k in range(chunks):
        sib_copy(k).wait_send()

        @pl.when(p > 0)
        def _():
            z_copy(k).wait_send()


def per_device(layer_inputs, out_grad, short_weights, long_filters, out_weights):
    sections, n, ntp = (lax.axis_size(a) for a in ("pipe", "seq", "tp"))
    m = n * ntp
    channels = layer_inputs.shape[2]
    tokens = layer_inputs.shape[1] * m
    cb = channels // m
    taps = short_weights.shape[1]
    width = long_filters.shape[2]
    groups = long_filters.shape[1] // n
    half = channels // ntp
    chunk = min(128, cb)
    chunks = cb // chunk
    dims = (sections, n, ntp, tokens, cb, groups, width, taps, chunk)
    tap_rows = jnp.pad(
        short_weights.reshape(taps * 3, half).astype(F32), ((0, TAP_ROWS - taps * 3), (0, 0))
    )
    dma = pltpu.SemaphoreType.DMA
    anywhere = pl.BlockSpec(memory_space=pl.ANY)
    input_grad, short_grad, long_grad = pl.pallas_call(
        functools.partial(kernel, dims),
        out_shape=(
            jax.ShapeDtypeStruct((tokens // n, half), BF16),
            jax.ShapeDtypeStruct((TAP_ROWS, half), F32),
            jax.ShapeDtypeStruct((groups * n, width), F32),
        ),
        in_specs=[anywhere] * 5,
        out_specs=(anywhere,) * 3,
        scratch_shapes=[
            pltpu.VMEM((tokens, cb), BF16),
            pltpu.VMEM((tokens, cb), BF16),
            pltpu.VMEM((TAP_ROWS, cb), F32),
            pltpu.VMEM((groups, width), F32),
            pltpu.VMEM((half, channels // n), BF16),
            pltpu.VMEM((cb, tokens), F32),
            pltpu.VMEM((cb, TAP_ROWS), F32),
            pltpu.VMEM((3, cb, tokens), F32),
            pltpu.VMEM((cb, tokens), F32),
            pltpu.VMEM((cb, tokens), F32),
            pltpu.VMEM((cb, tokens), BF16),
            pltpu.VMEM((cb, tokens), BF16),
            pltpu.VMEM((groups, width, 2 * width), BF16),
            pltpu.VMEM((ntp * cb, tokens), BF16),
            pltpu.VMEM((n, cb, tokens), BF16),
            pltpu.VMEM((n, cb, tokens), BF16),
            pltpu.VMEM((cb, tokens), BF16),
            pltpu.VMEM((tokens, cb), BF16),
            pltpu.VMEM((cb, TAP_ROWS), F32),
            pltpu.VMEM((TAP_ROWS, cb), F32),
            pltpu.VMEM((groups, width), F32),
            dma((m,)),
            dma((m,)),
            dma((n,)),
            dma((n,)),
            dma((2,)),
            dma((2,)),
            dma((chunks,)),
            dma((chunks,)),
            dma((chunks,)),
            dma((chunks,)),
            dma((chunks, n)),
            dma((chunks, n)),
            dma((n,)),
            dma((n,)),
            dma((n,)),
            dma((n,)),
            dma((n,)),
            dma((n,)),
            dma((8,)),
        ],
        compiler_params=pltpu.CompilerParams(
            collective_id=0, has_side_effects=True, vmem_limit_bytes=52 * 1024 * 1024
        ),
        name="sections_backward",
    )(layer_inputs[0], out_grad, tap_rows, long_filters[0].astype(F32), out_weights[0])
    short_result = short_grad[: taps * 3].reshape(1, taps, 3, half)
    return (input_grad[None], short_result, long_grad[None])


def solution(mesh):
    in_specs = (
        P("pipe", ("seq", "tp"), None),
        P("seq", "tp"),
        P("pipe", None, None, "tp"),
        P("pipe", "tp", None),
        P("pipe", "tp", "seq"),
    )
    out_specs = (P("pipe", "seq", "tp"), P("pipe", None, None, "tp"), P("pipe", "tp", None))
    return jax.shard_map(
        per_device, mesh=mesh, in_specs=in_specs, out_specs=out_specs, check_vma=False
    )
```

```python
import functools

import jax
import jax.numpy as jnp
from jax import lax
from jax.experimental import pallas as pl
from jax.experimental.pallas import tpu as pltpu
from jax.sharding import PartitionSpec as P

MESH = pl.DeviceIdType.MESH
F32 = jnp.float32
BF16 = jnp.bfloat16
TAP_ROWS = 32


def remote(src, dst, send_sem, recv_sem, device):
    return pltpu.make_async_remote_copy(
        src_ref=src,
        dst_ref=dst,
        send_sem=send_sem,
        recv_sem=recv_sem,
        device_id=device,
        device_id_type=MESH,
    )


def aligned(index, size):
    return pl.ds(pl.multiple_of(index * size, size), size)


def kernel(
    dims,
    x_hbm,
    og_hbm,
    taps_hbm,
    filt_hbm,
    w_hbm,
    ig_out,
    short_out,
    long_out,
    xin,
    gin,
    taps_in,
    filt,
    w_vmem,
    w_swap,
    gate_sum,
    xt,
    cols,
    feats,
    mixed,
    dkv,
    kv,
    dm,
    toep,
    gbuf,
    part,
    rs,
    ig,
    ot,
    short_cols,
    short_rows,
    long_rows,
    x_send,
    x_recv,
    og_send,
    og_recv,
    small_send,
    small_recv,
    sib_send,
    sib_recv,
    ag_send,
    ag_recv,
    ws_send,
    ws_recv,
    z_send,
    z_recv,
    rs_send,
    rs_recv,
    ig_send,
    ig_recv,
    sg_send,
    sg_recv,
    lg_send,
    lg_recv,
    local_sem,
):
    sections, n, nb, ntp, tokens, cb, groups, width, taps, chunk = dims
    na = n // nb
    halves = na // ntp
    chip = ntp * cb
    m = n * ntp
    chunks = cb // chunk
    blocks = tokens // width
    gw = cb // groups
    tl = tokens // n
    p, q, c = lax.axis_index("pipe"), lax.axis_index("seq"), lax.axis_index("tp")
    b = q * ntp + c
    half, slot = b // n, lax.rem(b, n)
    a, e = q // nb, lax.rem(q, nb)
    sibling = (p, q, 1 - c)
    owns = c == half
    last = p == sections - 1

    def place(block):
        return (p, block // ntp, lax.rem(block, ntp))

    barrier = pltpu.get_barrier_semaphore()
    for r in range(1, m):
        pl.semaphore_signal(
            barrier, inc=1, device_id=place(lax.rem(b + r, m)), device_id_type=MESH
        )

    @pl.when(p > 0)
    def _():
        pl.semaphore_signal(barrier, inc=1, device_id=(p - 1, q, c), device_id_type=MESH)

    @pl.when(p < sections - 1)
    def _():
        pl.semaphore_signal(barrier, inc=1, device_id=(p + 1, q, c), device_id_type=MESH)

    w_copy = pltpu.make_async_copy(w_hbm, w_vmem, local_sem.at[0])

    @pl.when(last)
    def _():
        w_copy.start()

    def swap_refs(h, to, source):
        rows = pl.ds(pl.multiple_of((h * nb + to) * chip, chip), chip)
        return w_hbm.at[rows], w_swap.at[pl.ds(h * chip, chip), aligned(source, chip)]

    def swap_own(h):
        src, dst = swap_refs(h, e, e)
        return pltpu.make_async_copy(src, dst, ws_send.at[0, h])

    def swap_copy(h, r):
        to = lax.rem(e + r, nb)
        src, dst = swap_refs(h, to, e)
        return remote(src, dst, ws_send.at[r, h], ws_recv.at[r, h], (p, a * nb + to, c))

    def swap_wait(h, r):
        source = lax.rem(e - r + nb, nb)
        src, dst = swap_refs(h, 0, source)
        remote(src, dst, ws_send.at[r, h], ws_recv.at[r, h], sibling).wait_recv()

    @pl.when(jnp.logical_not(last))
    def _():
        for h in range(halves):
            swap_own(h).start()

    x_rows = tokens // m
    x_local = pltpu.make_async_copy(
        x_hbm.at[:, aligned(b, cb)], xin.at[aligned(b, x_rows)], local_sem.at[1]
    )
    x_local.start()
    ends = (p > 0).astype(jnp.int32) + (p < sections - 1).astype(jnp.int32)
    pl.semaphore_wait(barrier, m - 1 + ends)

    def og_copy(j):
        block = c * n + j
        return block, remote(
            og_hbm.at[:, aligned(j, cb)],
            gin.at[aligned(q, tl)],
            og_send.at[j],
            og_recv.at[q],
            place(block),
        )

    @pl.when(last)
    def _():
        for j in range(n):
            block, copy = og_copy(j)

            @pl.when(block != b)
            def _():
                copy.start()

        @pl.when(owns)
        def _():
            own = pltpu.make_async_copy(
                og_hbm.at[:, aligned(slot, cb)], gin.at[aligned(q, tl)], local_sem.at[2]
            )
            own.start()
            own.wait()

    def x_copy(r):
        block = lax.rem(b + r, m)
        return remote(
            x_hbm.at[:, aligned(block, cb)],
            xin.at[aligned(b, x_rows)],
            x_send.at[r],
            x_recv.at[r],
            place(block),
        )

    for r in range(1, m):
        x_copy(r).start()

    other = lax.rem(q * ntp + 1 - c, n)
    taps_copy = remote(
        taps_hbm.at[:, aligned(other, cb)], taps_in, small_send.at[0], small_recv.at[0], sibling
    )
    filt_copy = remote(
        filt_hbm.at[aligned(other, groups)], filt, small_send.at[1], small_recv.at[1], sibling
    )

    @pl.when(owns)
    def _():
        taps_copy.start()
        filt_copy.start()
        taps_own = pltpu.make_async_copy(
            taps_hbm.at[:, aligned(slot, cb)], taps_in, local_sem.at[3]
        )
        filt_own = pltpu.make_async_copy(filt_hbm.at[aligned(slot, groups)], filt, local_sem.at[4])
        taps_own.start()
        filt_own.start()
        taps_own.wait()
        filt_own.wait()

    @pl.when(jnp.logical_not(last))
    def _():
        for r in range(1, nb):
            for h in range(halves):
                swap_copy(h, r).start()

    def grad_rows(from_e, core, k):
        return pl.ds(pl.multiple_of((from_e * ntp + core) * cb + k * chunk, chunk), chunk)

    def sib_copy(k, r, core=None):
        ref = gbuf.at[grad_rows(lax.rem(e - r + nb, nb), c if core is None else core, k)]
        return remote(ref, ref, sib_send.at[k, r], sib_recv.at[k, r], sibling)

    def ag_copy(k, r):
        ref = gbuf.at[grad_rows(e, c, k)]
        to = lax.rem(e + r, nb)
        return remote(ref, ref, ag_send.at[k, r], ag_recv.at[k, r], (p, a * nb + to, c))

    def ag_wait(k, r):
        ref = gbuf.at[grad_rows(lax.rem(e - r + nb, nb), c, k)]
        remote(ref, ref, ag_send.at[k, r], ag_recv.at[k, r], sibling).wait_recv()

    def span_of(k):
        return pl.ds(pl.multiple_of(k * chunk, chunk), chunk)

    def part_copy(j, k, block, source):
        rows = span_of(k)
        return remote(
            part.at[j, rows], rs.at[source, rows], rs_send.at[k, j], rs_recv.at[k, source], place(block)
        )

    def part_block_last(j):
        return c * n + j

    def part_block(j):
        return ((c * halves + j // ntp) * nb + e) * ntp + lax.rem(j, ntp)

    def dense(count, block_of, source, start, weight, grad):
        def one(step, carry):
            k, j = step // count, lax.rem(step + start, count)
            block = block_of(j)
            copy = part_copy(j, k, block, source)
            rows = span_of(k)
            w_rows = pl.ds(pl.multiple_of(j * cb + k * chunk, chunk), chunk)
            product = jnp.dot(
                weight[w_rows, :], grad[...], preferred_element_type=F32
            ).astype(BF16)

            @pl.when(block != b)
            def _():
                part[j, rows, :] = product
                copy.start()

            @pl.when(block == b)
            def _():
                rs[source, rows, :] = product

            return carry

        lax.fori_loop(0, chunks * count, one, 0)

    @pl.when(last)
    def _():
        for source in range(n):

            @pl.when(jnp.logical_or(source != q, jnp.logical_not(owns)))
            def _():
                remote(
                    og_hbm.at[:, pl.ds(0, cb)],
                    gin.at[pl.ds(source * tl, tl)],
                    og_send.at[0],
                    og_recv.at[source],
                    sibling,
                ).wait_recv()

        for k in range(chunks):
            gbuf[grad_rows(e, c, k), :] = (
                gin[:, pl.ds(k * chunk, chunk)].astype(F32).T.astype(BF16)
            )
            sib_copy(k, 0).start()
        w_copy.wait()
        for k in range(chunks):
            sib_copy(k, 0, 1 - c).wait_recv()
        dense(n, part_block_last, q, slot + 1, w_vmem, gbuf.at[aligned(e, chip)])

    x_local.wait()
    for r in range(1, m):
        source = lax.rem(b - r + m, m)
        remote(
            x_hbm.at[:, pl.ds(0, cb)],
            xin.at[aligned(source, x_rows)],
            x_send.at[r],
            x_recv.at[r],
            sibling,
        ).wait_recv()
    for k in range(chunks):
        span = pl.ds(k * chunk, chunk)
        xt[span, :] = xin[:, span].astype(F32).T

    @pl.when(jnp.logical_not(owns))
    def _():
        taps_copy.wait_recv()
        filt_copy.wait_recv()

    cols[...] = taps_in[...].T
    lane = lax.broadcasted_iota(jnp.int32, (gw, tokens), 1)

    def later(value, by):
        if by == 0:
            return value
        return jnp.where(lane >= by, pltpu.roll(value, by, 1), 0.0)

    def earlier(value, by):
        if by == 0:
            return value
        return jnp.where(lane < tokens - by, pltpu.roll(value, tokens - by, 1), 0.0)

    def stacked(value):
        return jnp.concatenate(
            [value[:, i * width : (i + 1) * width] for i in range(blocks)], axis=0
        )

    def windows(value):
        wide = jnp.concatenate([value, jnp.zeros((gw, width), value.dtype)], axis=1)
        return jnp.concatenate(
            [wide[:, i * width : (i + 2) * width] for i in range(blocks)], axis=0
        )

    def group_rows(g):
        return aligned(g, gw)

    def grad_rows16(g):
        return pl.ds(pl.multiple_of((e * ntp + c) * cb + g * gw, gw), gw)

    def recompute(g, carry):
        rows = group_rows(g)
        source = xt[rows, :]
        weight = cols[rows, :]
        running = [jnp.zeros((gw, tokens), F32)] * 3
        for j in range(taps):
            shifted = later(source, j)
            for f in range(3):
                running[f] = running[f] + weight[:, 3 * j + f : 3 * j + f + 1] * shifted
        for f in range(3):
            feats[f, rows, :] = running[f]
        product = (running[1] * running[2]).astype(BF16)
        kv[rows, :] = product
        tap_row = jnp.concatenate([filt[pl.ds(g, 1), :], jnp.zeros((1, width), F32)], axis=1)
        band = pltpu.roll(
            jnp.broadcast_to(tap_row, (width, 2 * width)), 0, 1, stride=1, stride_axis=0
        ).astype(BF16)
        toep[g] = band
        spread = jnp.dot(stacked(product), band, preferred_element_type=F32)
        for i in range(blocks):
            value = spread[i * gw : (i + 1) * gw, :width]
            if i > 0:
                value = value + spread[(i - 1) * gw : i * gw, width:]
            mixed[rows, pl.ds(i * width, width)] = value
        return carry

    lax.fori_loop(0, groups, recompute, 0, unroll=2)

    def z_copy(k):
        return remote(
            ig.at[span_of(k)],
            gbuf.at[grad_rows(e, c, k)],
            z_send.at[k],
            z_recv.at[k],
            (jnp.maximum(p - 1, 0), q, c),
        )

    @pl.when(jnp.logical_not(last))
    def _():
        def hand_on(k):
            for r in range(1, nb):
                ag_wait(k, r)
                sib_copy(k, r).start()

        for k in range(chunks):
            z_copy(k).wait_recv()
            for r in range(1, nb):
                ag_copy(k, r).start()
            sib_copy(k, 0).start()
            if k > 0:
                hand_on(k - 1)
        hand_on(chunks - 1)
        for h in range(halves):
            swap_own(h).wait()
            for r in range(1, nb):
                swap_wait(h, r)
        for k in range(chunks):
            for r in range(nb):
                sib_copy(k, r, 1 - c).wait_recv()
        dense(na, part_block, a, 0, w_swap, gbuf)

    def backward(g, carry):
        rows = group_rows(g)
        gate = gate_sum[rows, :].astype(F32)
        mixed_grad = (gate * feats[0, rows, :]).astype(BF16)
        dm[rows, :] = mixed_grad
        result = lax.dot_general(
            windows(mixed_grad), toep[g], (((1,), (1,)), ((), ())), preferred_element_type=F32
        )
        product_grad = jnp.concatenate(
            [result[i * gw : (i + 1) * gw] for i in range(blocks)], axis=1
        )
        dkv[rows, :] = product_grad
        query_grad = gate * mixed[rows, :]
        mixed[rows, :] = query_grad
        grads = (query_grad, product_grad * feats[2, rows, :], product_grad * feats[1, rows, :])
        weight = cols[rows, :]
        total = gbuf[grad_rows16(g), :].astype(F32)
        for j in range(taps):
            term = weight[:, 3 * j : 3 * j + 1] * grads[0]
            for f in (1, 2):
                term = term + weight[:, 3 * j + f : 3 * j + f + 1] * grads[f]
            total = total + earlier(term, j)
        ig[rows, :] = total.astype(BF16)
        return carry

    per_chunk = chunk // gw

    def chunk_groups(k, body):
        lax.fori_loop(0, per_chunk, lambda i, carry: body(k * per_chunk + i, carry), 0, unroll=2)

    def arrived(k, count, self_source):
        rows = span_of(k)
        for source in range(count):

            @pl.when(jnp.logical_or(source != self_source, jnp.logical_not(owns)))
            def _():
                remote(
                    part.at[0, rows],
                    rs.at[source, rows],
                    rs_send.at[k, 0],
                    rs_recv.at[k, source],
                    sibling,
                ).wait_recv()

        def add(g, carry):
            part_rows = group_rows(g)
            total = rs[0, part_rows, :].astype(F32)
            for source in range(1, count):
                total = total + rs[source, part_rows, :].astype(F32)
            gate_sum[part_rows, :] = total.astype(BF16)
            return carry

        chunk_groups(k, add)

    def give(src, dst, send_sem, recv_sem, target):
        copy = remote(src, dst, send_sem, recv_sem, (p, target, half))
        own = pltpu.make_async_copy(src, dst, send_sem)
        away = jnp.logical_or(target != q, jnp.logical_not(owns))

        def start():
            pl.when(away)(copy.start)
            pl.when(jnp.logical_not(away))(own.start)

        def sent():
            pl.when(away)(copy.wait_send)
            pl.when(jnp.logical_not(away))(own.wait)

        return start, sent

    def ig_give(target, k):
        columns = pl.ds(pl.multiple_of(slot * cb + k * chunk, chunk), chunk)
        return give(
            ot.at[pl.ds(target * tl, tl), span_of(k)],
            ig_out.at[:, columns],
            ig_send.at[k, target],
            ig_recv.at[k, slot],
            target,
        )

    def short_give(target):
        return give(
            short_rows,
            short_out.at[:, aligned(slot, cb)],
            sg_send.at[target],
            sg_recv.at[slot],
            target,
        )

    def long_give(target):
        return give(
            long_rows,
            long_out.at[aligned(slot, groups)],
            lg_send.at[target],
            lg_recv.at[slot],
            target,
        )

    def out_chunk(k):
        span = span_of(k)
        ot[:, span] = ig[span, :].astype(F32).T.astype(BF16)
        for target in range(n):
            ig_give(target, k)[0]()

    column = lax.broadcasted_iota(jnp.int32, (gw, TAP_ROWS), 1)
    low = lax.broadcasted_iota(jnp.int32, (8, 2 * width), 0)

    def filters(g, carry):
        rows = group_rows(g)
        source = xt[rows, :]
        product_grad = dkv[rows, :]
        grads = (
            mixed[rows, :],
            product_grad * feats[2, rows, :],
            product_grad * feats[1, rows, :],
        )
        sums = jnp.zeros((gw, TAP_ROWS), F32)
        for j in range(taps):
            shifted = later(source, j)
            for f in range(3):
                total = jnp.sum(grads[f] * shifted, axis=1, keepdims=True)
                sums = jnp.where(column == 3 * j + f, total, sums)
        short_cols[rows, :] = sums
        lags = lax.dot_general(
            stacked(kv[rows, :]),
            windows(dm[rows, :]),
            (((0,), (0,)), ((), ())),
            preferred_element_type=F32,
        )
        size = width
        while size > 8:
            size //= 2
            lags = lags[:size] + pltpu.roll(lags[size:], 2 * width - size, 1)
        for bit in (4, 2, 1):
            lags = jnp.where((low & bit) != 0, pltpu.roll(lags, 2 * width - bit, 1), lags)
        long_rows[pl.ds(g, 1), :] = jnp.sum(lags, axis=0, keepdims=True)[:, :width]
        return carry

    def section_step(k, carry):
        @pl.when(last)
        def _():
            arrived(k, n, q)

        @pl.when(jnp.logical_not(last))
        def _():
            arrived(k, na, a)

        chunk_groups(k, backward)

        @pl.when(p > 0)
        def _():
            z_copy(k).start()

        @pl.when(p == 0)
        def _():
            out_chunk(k)
            chunk_groups(k, filters)

        return carry

    lax.fori_loop(0, chunks, section_step, 0)

    @pl.when(p > 0)
    def _():
        def finish(k, carry):
            out_chunk(k)
            chunk_groups(k, filters)
            return carry

        lax.fori_loop(0, chunks, finish, 0)

    short_rows[...] = short_cols[...].T
    for target in range(n):
        short_give(target)[0]()
        long_give(target)[0]()

    for j in range(n):

        @pl.when(c * n + j != b)
        def _():
            for k in range(chunks):
                remote(
                    ot.at[pl.ds(0, tl), pl.ds(0, chunk)],
                    ig_out.at[:, pl.ds(j * cb + k * chunk, chunk)],
                    ig_send.at[k, 0],
                    ig_recv.at[k, j],
                    sibling,
                ).wait_recv()
            for src, dst, send, recv in (
                (short_rows, short_out.at[:, pl.ds(j * cb, cb)], sg_send, sg_recv),
                (long_rows, long_out.at[pl.ds(j * groups, groups)], lg_send, lg_recv),
            ):
                remote(src, dst, send.at[0], recv.at[j], sibling).wait_recv()

    for target in range(n):
        short_give(target)[1]()
        long_give(target)[1]()
        for k in range(chunks):
            ig_give(target, k)[1]()
    for r in range(1, m):
        x_copy(r).wait_send()

    @pl.when(owns)
    def _():
        taps_copy.wait_send()
        filt_copy.wait_send()

    @pl.when(last)
    def _():
        for j in range(n):
            block, copy = og_copy(j)

            @pl.when(block != b)
            def _():
                copy.wait_send()
                for k in range(chunks):
                    part_copy(j, k, block, q).wait_send()

    @pl.when(jnp.logical_not(last))
    def _():
        for j in range(na):
            block = part_block(j)

            @pl.when(block != b)
            def _():
                for k in range(chunks):
                    part_copy(j, k, block, a).wait_send()

        for r in range(1, nb):
            for h in range(halves):
                swap_copy(h, r).wait_send()
            for k in range(chunks):
                ag_copy(k, r).wait_send()
                sib_copy(k, r).wait_send()

    for k in range(chunks):
        sib_copy(k, 0).wait_send()

        @pl.when(p > 0)
        def _():
            z_copy(k).wait_send()


def per_device(layer_inputs, out_grad, short_weights, long_filters, out_weights):
    sections, n, ntp = (lax.axis_size(a) for a in ("pipe", "seq", "tp"))
    m = n * ntp
    channels = layer_inputs.shape[2]
    tokens = layer_inputs.shape[1] * m
    cb = channels // m
    taps = short_weights.shape[1]
    width = long_filters.shape[2]
    groups = long_filters.shape[1] // n
    half = channels // ntp
    chunk = min(128, cb)
    chunks = cb // chunk
    nb = max(d for d in range(1, n + 1) if n % d == 0 and d * d <= n)
    halves = n // nb // ntp
    dims = (sections, n, nb, ntp, tokens, cb, groups, width, taps, chunk)
    tap_rows = jnp.pad(
        short_weights.reshape(taps * 3, half).astype(F32), ((0, TAP_ROWS - taps * 3), (0, 0))
    )
    dma = pltpu.SemaphoreType.DMA
    anywhere = pl.BlockSpec(memory_space=pl.ANY)
    input_grad, short_grad, long_grad = pl.pallas_call(
        functools.partial(kernel, dims),
        out_shape=(
            jax.ShapeDtypeStruct((tokens // n, half), BF16),
            jax.ShapeDtypeStruct((TAP_ROWS, half), F32),
            jax.ShapeDtypeStruct((groups * n, width), F32),
        ),
        in_specs=[anywhere] * 5,
        out_specs=(anywhere,) * 3,
        scratch_shapes=[
            pltpu.VMEM((tokens, cb), BF16),
            pltpu.VMEM((tokens, cb), BF16),
            pltpu.VMEM((TAP_ROWS, cb), F32),
            pltpu.VMEM((groups, width), F32),
            pltpu.VMEM((half, channels // n), BF16),
            pltpu.VMEM((half // nb, channels // n * nb), BF16),
            pltpu.VMEM((cb, tokens), BF16),
            pltpu.VMEM((cb, tokens), F32),
            pltpu.VMEM((cb, TAP_ROWS), F32),
            pltpu.VMEM((3, cb, tokens), F32),
            pltpu.VMEM((cb, tokens), F32),
            pltpu.VMEM((cb, tokens), F32),
            pltpu.VMEM((cb, tokens), BF16),
            pltpu.VMEM((cb, tokens), BF16),
            pltpu.VMEM((groups, width, 2 * width), BF16),
            pltpu.VMEM((nb * ntp * cb, tokens), BF16),
            pltpu.VMEM((n, cb, tokens), BF16),
            pltpu.VMEM((n, cb, tokens), BF16),
            pltpu.VMEM((cb, tokens), BF16),
            pltpu.VMEM((tokens, cb), BF16),
            pltpu.VMEM((cb, TAP_ROWS), F32),
            pltpu.VMEM((TAP_ROWS, cb), F32),
            pltpu.VMEM((groups, width), F32),
            dma((m,)),
            dma((m,)),
            dma((n,)),
            dma((n,)),
            dma((2,)),
            dma((2,)),
            dma((chunks, nb)),
            dma((chunks, nb)),
            dma((chunks, nb)),
            dma((chunks, nb)),
            dma((nb, halves)),
            dma((nb, halves)),
            dma((chunks,)),
            dma((chunks,)),
            dma((chunks, n)),
            dma((chunks, n)),
            dma((chunks, n)),
            dma((chunks, n)),
            dma((n,)),
            dma((n,)),
            dma((n,)),
            dma((n,)),
            dma((8,)),
        ],
        compiler_params=pltpu.CompilerParams(
            collective_id=0, has_side_effects=True, vmem_limit_bytes=52 * 1024 * 1024
        ),
        name="sections_backward",
    )(layer_inputs[0], out_grad, tap_rows, long_filters[0].astype(F32), out_weights[0])
    short_result = short_grad[: taps * 3].reshape(1, taps, 3, half)
    return (input_grad[None], short_result, long_grad[None])


def solution(mesh):
    in_specs = (
        P("pipe", ("seq", "tp"), None),
        P("seq", "tp"),
        P("pipe", None, None, "tp"),
        P("pipe", "tp", None),
        P("pipe", "tp", "seq"),
    )
    out_specs = (P("pipe", "seq", "tp"), P("pipe", None, None, "tp"), P("pipe", "tp", None))
    return jax.shard_map(
        per_device, mesh=mesh, in_specs=in_specs, out_specs=out_specs, check_vma=False
    )
```

```python
import functools

import jax
import jax.numpy as jnp
from jax import lax
from jax.experimental import pallas as pl
from jax.experimental.pallas import tpu as pltpu
from jax.sharding import PartitionSpec as P

MESH = pl.DeviceIdType.MESH
F32 = jnp.float32
BF16 = jnp.bfloat16
TAP_ROWS = 32


def remote(src, dst, send_sem, recv_sem, device):
    return pltpu.make_async_remote_copy(
        src_ref=src,
        dst_ref=dst,
        send_sem=send_sem,
        recv_sem=recv_sem,
        device_id=device,
        device_id_type=MESH,
    )


def aligned(index, size):
    return pl.ds(pl.multiple_of(index * size, size), size)


def kernel(
    dims,
    x_hbm,
    og_hbm,
    taps_hbm,
    filt_hbm,
    w_hbm,
    ig_out,
    short_out,
    long_out,
    xin,
    gin,
    taps_in,
    filt,
    w_vmem,
    w_swap,
    gate_sum,
    xt,
    cols,
    feats,
    mixed,
    dkv,
    kv,
    dm,
    toep,
    gbuf,
    part,
    rs,
    ig,
    ot,
    short_cols,
    short_rows,
    long_rows,
    x_send,
    x_recv,
    og_send,
    og_recv,
    small_send,
    small_recv,
    ag_send,
    ag_recv,
    ws_send,
    ws_recv,
    z_send,
    z_recv,
    rs_send,
    rs_recv,
    ig_send,
    ig_recv,
    sg_send,
    sg_recv,
    lg_send,
    lg_recv,
    local_sem,
):
    sections, n, nb, ntp, tokens, cb, groups, width, taps, chunk = dims
    halves = nb // ntp
    chip = ntp * cb
    m = n * ntp
    chunks = cb // chunk
    blocks = tokens // width
    gw = cb // groups
    tl = tokens // n
    p, q, c = lax.axis_index("pipe"), lax.axis_index("seq"), lax.axis_index("tp")
    b = q * ntp + c
    half, slot = b // n, lax.rem(b, n)
    a, e = q // nb, lax.rem(q, nb)
    u, v = jnp.where(c == 0, a, e), jnp.where(c == 0, e, a)
    sibling = (p, q, 1 - c)
    owns = c == half
    last = p == sections - 1

    def place(block):
        return (p, block // ntp, lax.rem(block, ntp))

    barrier = pltpu.get_barrier_semaphore()
    for r in range(1, m):
        pl.semaphore_signal(
            barrier, inc=1, device_id=place(lax.rem(b + r, m)), device_id_type=MESH
        )

    @pl.when(p > 0)
    def _():
        pl.semaphore_signal(barrier, inc=1, device_id=(p - 1, q, c), device_id_type=MESH)

    @pl.when(p < sections - 1)
    def _():
        pl.semaphore_signal(barrier, inc=1, device_id=(p + 1, q, c), device_id_type=MESH)

    w_copy = pltpu.make_async_copy(w_hbm, w_vmem, local_sem.at[0])

    @pl.when(last)
    def _():
        w_copy.start()

    def swap_pieces():
        for i in range(halves):
            for j in range(nb):
                to, row = j, c * halves + i
                yield 0, i * nb + j, a * nb + to, row, row * nb + to, e
                to, row = c * halves + i, j
                yield 1, i * nb + j, to * nb + e, row, to * nb + row, a

    def swap_copies(piece):
        core, index, chip_to, row, owner, column = piece
        local = owner - c * (n // ntp)
        src = w_hbm.at[pl.ds(pl.multiple_of(local * chip + core * cb, cb), cb)]
        dst = w_swap.at[aligned(row, cb), aligned(column, chip)]
        send = ws_send.at[core, index]
        far = remote(src, dst, send, ws_recv.at[row * nb + column], (p, chip_to, core))
        near = pltpu.make_async_copy(src, dst, send)
        return jnp.logical_or(chip_to != q, core != c), far, near

    def swap_start():
        for piece in swap_pieces():
            away, far, near = swap_copies(piece)
            pl.when(away)(far.start)
            pl.when(jnp.logical_not(away))(near.start)

    def swap_sent():
        for piece in swap_pieces():
            away, far, near = swap_copies(piece)
            pl.when(away)(far.wait_send)

    def swap_arrived():
        for piece in swap_pieces():
            away, far, near = swap_copies(piece)
            pl.when(jnp.logical_not(away))(near.wait)
        for row in range(nb):
            owner = jnp.where(c == 0, row * nb + v, v * nb + row)
            for column in range(nb):
                away = jnp.logical_or(column != v, owner // (n // ntp) != c)
                far = remote(
                    w_hbm.at[pl.ds(0, cb)],
                    w_swap.at[pl.ds(row * cb, cb), pl.ds(column * chip, chip)],
                    ws_send.at[0, 0],
                    ws_recv.at[row * nb + column],
                    sibling,
                )
                pl.when(away)(far.wait_recv)

    x_rows = tokens // m
    x_local = pltpu.make_async_copy(
        x_hbm.at[:, aligned(b, cb)], xin.at[aligned(b, x_rows)], local_sem.at[1]
    )
    x_local.start()
    ends = (p > 0).astype(jnp.int32) + (p < sections - 1).astype(jnp.int32)
    pl.semaphore_wait(barrier, m - 1 + ends)

    def og_copy(j):
        block = c * n + j
        return block, remote(
            og_hbm.at[:, aligned(j, cb)],
            gin.at[aligned(q, tl)],
            og_send.at[j],
            og_recv.at[q],
            place(block),
        )

    @pl.when(last)
    def _():
        for j in range(n):
            block, copy = og_copy(j)

            @pl.when(block != b)
            def _():
                copy.start()

        @pl.when(owns)
        def _():
            own = pltpu.make_async_copy(
                og_hbm.at[:, aligned(slot, cb)], gin.at[aligned(q, tl)], local_sem.at[2]
            )
            own.start()
            own.wait()

    def x_copy(r):
        block = lax.rem(b + r, m)
        return remote(
            x_hbm.at[:, aligned(block, cb)],
            xin.at[aligned(b, x_rows)],
            x_send.at[r],
            x_recv.at[r],
            place(block),
        )

    for r in range(1, m):
        x_copy(r).start()

    other = lax.rem(q * ntp + 1 - c, n)
    taps_copy = remote(
        taps_hbm.at[:, aligned(other, cb)], taps_in, small_send.at[0], small_recv.at[0], sibling
    )
    filt_copy = remote(
        filt_hbm.at[aligned(other, groups)], filt, small_send.at[1], small_recv.at[1], sibling
    )

    @pl.when(owns)
    def _():
        taps_copy.start()
        filt_copy.start()
        taps_own = pltpu.make_async_copy(
            taps_hbm.at[:, aligned(slot, cb)], taps_in, local_sem.at[3]
        )
        filt_own = pltpu.make_async_copy(filt_hbm.at[aligned(slot, groups)], filt, local_sem.at[4])
        taps_own.start()
        filt_own.start()
        taps_own.wait()
        filt_own.wait()

    pl.when(jnp.logical_not(last))(swap_start)

    def grad_rows(at, core, k):
        return pl.ds(pl.multiple_of((at * ntp + core) * cb + k * chunk, chunk), chunk)

    def gather_copy(k, index, at, device):
        return remote(
            gbuf.at[grad_rows(v, c, k)],
            gbuf.at[grad_rows(at, c, k)],
            ag_send.at[k, index],
            ag_recv.at[k, at * ntp + c],
            device,
        )

    def sib_copy(k):
        return gather_copy(k, 0, u, sibling)

    def gather_copies(k):
        copies = []
        for r in range(1, nb):
            to = lax.rem(e + r, nb)
            copies.append(gather_copy(k, r, e, (p, a * nb + to, 0)))
            to = lax.rem(a + r, nb)
            copies.append(gather_copy(k, nb - 1 + r, a, (p, to * nb + e, 1)))
        return copies

    def gather_wait(k, at, core):
        ref = gbuf.at[grad_rows(at, core, k)]
        remote(ref, ref, ag_send.at[k, 0], ag_recv.at[k, at * ntp + core], sibling).wait_recv()

    def span_of(k):
        return pl.ds(pl.multiple_of(k * chunk, chunk), chunk)

    def part_copy(j, k, block, source):
        rows = span_of(k)
        return remote(
            part.at[j, rows], rs.at[source, rows], rs_send.at[k, j], rs_recv.at[k, source], place(block)
        )

    def part_block_last(j):
        return c * n + j

    def part_block(j):
        return jnp.where(c == 0, j * nb + v, v * nb + j) * ntp + c

    def dense(count, block_of, source, start, weight, grad):
        def one(step, carry):
            k, j = step // count, lax.rem(step + start, count)
            block = block_of(j)
            copy = part_copy(j, k, block, source)
            rows = span_of(k)
            w_rows = pl.ds(pl.multiple_of(j * cb + k * chunk, chunk), chunk)
            product = jnp.dot(
                weight[w_rows, :], grad[...], preferred_element_type=F32
            ).astype(BF16)

            @pl.when(block != b)
            def _():
                part[j, rows, :] = product
                copy.start()

            @pl.when(block == b)
            def _():
                rs[source, rows, :] = product

            return carry

        lax.fori_loop(0, chunks * count, one, 0)

    @pl.when(last)
    def _():
        for source in range(n):

            @pl.when(jnp.logical_or(source != q, jnp.logical_not(owns)))
            def _():
                remote(
                    og_hbm.at[:, pl.ds(0, cb)],
                    gin.at[pl.ds(source * tl, tl)],
                    og_send.at[0],
                    og_recv.at[source],
                    sibling,
                ).wait_recv()

        for k in range(chunks):
            gbuf[grad_rows(v, c, k), :] = (
                gin[:, pl.ds(k * chunk, chunk)].astype(F32).T.astype(BF16)
            )
            sib_copy(k).start()
        w_copy.wait()
        for k in range(chunks):
            gather_wait(k, v, 1 - c)
        dense(n, part_block_last, q, slot + 1, w_vmem, gbuf.at[aligned(v, chip)])

    x_local.wait()
    for r in range(1, m):
        source = lax.rem(b - r + m, m)
        remote(
            x_hbm.at[:, pl.ds(0, cb)],
            xin.at[aligned(source, x_rows)],
            x_send.at[r],
            x_recv.at[r],
            sibling,
        ).wait_recv()
    for k in range(chunks):
        span = pl.ds(k * chunk, chunk)
        xt[span, :] = xin[:, span].astype(F32).T

    @pl.when(jnp.logical_not(owns))
    def _():
        taps_copy.wait_recv()
        filt_copy.wait_recv()

    cols[...] = taps_in[...].T
    lane = lax.broadcasted_iota(jnp.int32, (gw, tokens), 1)

    def later(value, by):
        if by == 0:
            return value
        return jnp.where(lane >= by, pltpu.roll(value, by, 1), 0.0)

    def earlier(value, by):
        if by == 0:
            return value
        return jnp.where(lane < tokens - by, pltpu.roll(value, tokens - by, 1), 0.0)

    def stacked(value):
        return jnp.concatenate(
            [value[:, i * width : (i + 1) * width] for i in range(blocks)], axis=0
        )

    def windows(value):
        wide = jnp.concatenate([value, jnp.zeros((gw, width), value.dtype)], axis=1)
        return jnp.concatenate(
            [wide[:, i * width : (i + 2) * width] for i in range(blocks)], axis=0
        )

    def group_rows(g):
        return aligned(g, gw)

    def grad_rows16(g):
        return pl.ds(pl.multiple_of((v * ntp + c) * cb + g * gw, gw), gw)

    def recompute(g, carry):
        rows = group_rows(g)
        source = xt[rows, :]
        weight = cols[rows, :]
        running = [jnp.zeros((gw, tokens), F32)] * 3
        for j in range(taps):
            shifted = later(source, j)
            for f in range(3):
                running[f] = running[f] + weight[:, 3 * j + f : 3 * j + f + 1] * shifted
        for f in range(3):
            feats[f, rows, :] = running[f]
        product = (running[1] * running[2]).astype(BF16)
        kv[rows, :] = product
        tap_row = jnp.concatenate([filt[pl.ds(g, 1), :], jnp.zeros((1, width), F32)], axis=1)
        band = pltpu.roll(
            jnp.broadcast_to(tap_row, (width, 2 * width)), 0, 1, stride=1, stride_axis=0
        ).astype(BF16)
        toep[g] = band
        spread = jnp.dot(stacked(product), band, preferred_element_type=F32)
        for i in range(blocks):
            value = spread[i * gw : (i + 1) * gw, :width]
            if i > 0:
                value = value + spread[(i - 1) * gw : i * gw, width:]
            mixed[rows, pl.ds(i * width, width)] = value
        return carry

    lax.fori_loop(0, groups, recompute, 0, unroll=2)

    def z_copy(k):
        return remote(
            ig.at[span_of(k)],
            gbuf.at[grad_rows(v, c, k)],
            z_send.at[k],
            z_recv.at[k],
            (jnp.maximum(p - 1, 0), q, c),
        )

    @pl.when(jnp.logical_not(last))
    def _():
        for k in range(chunks):
            z_copy(k).wait_recv()
            for copy in gather_copies(k):
                copy.start()
            sib_copy(k).start()
        swap_arrived()
        for k in range(chunks):
            gather_wait(k, v, 1 - c)
            for r in range(1, nb):
                for core in range(ntp):
                    gather_wait(k, lax.rem(v + r, nb), core)
        dense(nb, part_block, u, u + 1, w_swap, gbuf)

    def backward(g, carry):
        rows = group_rows(g)
        gate = gate_sum[rows, :].astype(F32)
        mixed_grad = (gate * feats[0, rows, :]).astype(BF16)
        dm[rows, :] = mixed_grad
        result = lax.dot_general(
            windows(mixed_grad), toep[g], (((1,), (1,)), ((), ())), preferred_element_type=F32
        )
        product_grad = jnp.concatenate(
            [result[i * gw : (i + 1) * gw] for i in range(blocks)], axis=1
        )
        dkv[rows, :] = product_grad
        query_grad = gate * mixed[rows, :]
        mixed[rows, :] = query_grad
        grads = (query_grad, product_grad * feats[2, rows, :], product_grad * feats[1, rows, :])
        weight = cols[rows, :]
        total = gbuf[grad_rows16(g), :].astype(F32)
        for j in range(taps):
            term = weight[:, 3 * j : 3 * j + 1] * grads[0]
            for f in (1, 2):
                term = term + weight[:, 3 * j + f : 3 * j + f + 1] * grads[f]
            total = total + earlier(term, j)
        ig[rows, :] = total.astype(BF16)
        return carry

    per_chunk = chunk // gw

    def chunk_groups(k, body):
        lax.fori_loop(0, per_chunk, lambda i, carry: body(k * per_chunk + i, carry), 0, unroll=2)

    def arrived(k, count, self_source, kept):
        rows = span_of(k)
        for source in range(count):

            @pl.when(jnp.logical_or(source != self_source, jnp.logical_not(kept)))
            def _():
                remote(
                    part.at[0, rows],
                    rs.at[source, rows],
                    rs_send.at[k, 0],
                    rs_recv.at[k, source],
                    sibling,
                ).wait_recv()

        def add(g, carry):
            part_rows = group_rows(g)
            total = rs[0, part_rows, :].astype(F32)
            for source in range(1, count):
                total = total + rs[source, part_rows, :].astype(F32)
            gate_sum[part_rows, :] = total.astype(BF16)
            return carry

        chunk_groups(k, add)

    def give(src, dst, send_sem, recv_sem, target):
        copy = remote(src, dst, send_sem, recv_sem, (p, target, half))
        own = pltpu.make_async_copy(src, dst, send_sem)
        away = jnp.logical_or(target != q, jnp.logical_not(owns))

        def start():
            pl.when(away)(copy.start)
            pl.when(jnp.logical_not(away))(own.start)

        def sent():
            pl.when(away)(copy.wait_send)
            pl.when(jnp.logical_not(away))(own.wait)

        return start, sent

    def ig_give(target, k):
        columns = pl.ds(pl.multiple_of(slot * cb + k * chunk, chunk), chunk)
        return give(
            ot.at[pl.ds(target * tl, tl), span_of(k)],
            ig_out.at[:, columns],
            ig_send.at[k, target],
            ig_recv.at[k, slot],
            target,
        )

    def short_give(target):
        return give(
            short_rows,
            short_out.at[:, aligned(slot, cb)],
            sg_send.at[target],
            sg_recv.at[slot],
            target,
        )

    def long_give(target):
        return give(
            long_rows,
            long_out.at[aligned(slot, groups)],
            lg_send.at[target],
            lg_recv.at[slot],
            target,
        )

    def out_chunk(k):
        span = span_of(k)
        ot[:, span] = ig[span, :].astype(F32).T.astype(BF16)
        for target in range(n):
            ig_give(target, k)[0]()

    column = lax.broadcasted_iota(jnp.int32, (gw, TAP_ROWS), 1)
    low = lax.broadcasted_iota(jnp.int32, (8, 2 * width), 0)

    def filters(g, carry):
        rows = group_rows(g)
        source = xt[rows, :]
        product_grad = dkv[rows, :]
        grads = (
            mixed[rows, :],
            product_grad * feats[2, rows, :],
            product_grad * feats[1, rows, :],
        )
        sums = jnp.zeros((gw, TAP_ROWS), F32)
        for j in range(taps):
            shifted = later(source, j)
            for f in range(3):
                total = jnp.sum(grads[f] * shifted, axis=1, keepdims=True)
                sums = jnp.where(column == 3 * j + f, total, sums)
        short_cols[rows, :] = sums
        lags = lax.dot_general(
            stacked(kv[rows, :]),
            windows(dm[rows, :]),
            (((0,), (0,)), ((), ())),
            preferred_element_type=F32,
        )
        size = width
        while size > 8:
            size //= 2
            lags = lags[:size] + pltpu.roll(lags[size:], 2 * width - size, 1)
        for bit in (4, 2, 1):
            lags = jnp.where((low & bit) != 0, pltpu.roll(lags, 2 * width - bit, 1), lags)
        long_rows[pl.ds(g, 1), :] = jnp.sum(lags, axis=0, keepdims=True)[:, :width]
        return carry

    def section_step(k, carry):
        @pl.when(last)
        def _():
            arrived(k, n, q, owns)

        @pl.when(jnp.logical_not(last))
        def _():
            arrived(k, nb, u, True)

        chunk_groups(k, backward)

        @pl.when(p > 0)
        def _():
            z_copy(k).start()

        @pl.when(p == 0)
        def _():
            out_chunk(k)
            chunk_groups(k, filters)

        return carry

    lax.fori_loop(0, chunks, section_step, 0)

    @pl.when(p > 0)
    def _():
        def finish(k, carry):
            out_chunk(k)
            chunk_groups(k, filters)
            return carry

        lax.fori_loop(0, chunks, finish, 0)

    short_rows[...] = short_cols[...].T
    for target in range(n):
        short_give(target)[0]()
        long_give(target)[0]()

    for j in range(n):

        @pl.when(c * n + j != b)
        def _():
            for k in range(chunks):
                remote(
                    ot.at[pl.ds(0, tl), pl.ds(0, chunk)],
                    ig_out.at[:, pl.ds(j * cb + k * chunk, chunk)],
                    ig_send.at[k, 0],
                    ig_recv.at[k, j],
                    sibling,
                ).wait_recv()
            for src, dst, send, recv in (
                (short_rows, short_out.at[:, pl.ds(j * cb, cb)], sg_send, sg_recv),
                (long_rows, long_out.at[pl.ds(j * groups, groups)], lg_send, lg_recv),
            ):
                remote(src, dst, send.at[0], recv.at[j], sibling).wait_recv()

    for target in range(n):
        short_give(target)[1]()
        long_give(target)[1]()
        for k in range(chunks):
            ig_give(target, k)[1]()
    for r in range(1, m):
        x_copy(r).wait_send()

    @pl.when(owns)
    def _():
        taps_copy.wait_send()
        filt_copy.wait_send()

    @pl.when(last)
    def _():
        for j in range(n):
            block, copy = og_copy(j)

            @pl.when(block != b)
            def _():
                copy.wait_send()
                for k in range(chunks):
                    part_copy(j, k, block, q).wait_send()

    @pl.when(jnp.logical_not(last))
    def _():
        for j in range(nb):
            block = part_block(j)

            @pl.when(block != b)
            def _():
                for k in range(chunks):
                    part_copy(j, k, block, u).wait_send()

        swap_sent()
        for k in range(chunks):
            for copy in gather_copies(k):
                copy.wait_send()

    for k in range(chunks):
        sib_copy(k).wait_send()

        @pl.when(p > 0)
        def _():
            z_copy(k).wait_send()


def per_device(layer_inputs, out_grad, short_weights, long_filters, out_weights):
    sections, n, ntp = (lax.axis_size(a) for a in ("pipe", "seq", "tp"))
    m = n * ntp
    channels = layer_inputs.shape[2]
    tokens = layer_inputs.shape[1] * m
    cb = channels // m
    taps = short_weights.shape[1]
    width = long_filters.shape[2]
    groups = long_filters.shape[1] // n
    half = channels // ntp
    chunk = min(128, cb)
    chunks = cb // chunk
    nb = max(d for d in range(1, n + 1) if d * d <= n)
    assert nb * nb == n and nb % ntp == 0
    halves = nb // ntp
    dims = (sections, n, nb, ntp, tokens, cb, groups, width, taps, chunk)
    tap_rows = jnp.pad(
        short_weights.reshape(taps * 3, half).astype(F32), ((0, TAP_ROWS - taps * 3), (0, 0))
    )
    dma = pltpu.SemaphoreType.DMA
    anywhere = pl.BlockSpec(memory_space=pl.ANY)
    input_grad, short_grad, long_grad = pl.pallas_call(
        functools.partial(kernel, dims),
        out_shape=(
            jax.ShapeDtypeStruct((tokens // n, half), BF16),
            jax.ShapeDtypeStruct((TAP_ROWS, half), F32),
            jax.ShapeDtypeStruct((groups * n, width), F32),
        ),
        in_specs=[anywhere] * 5,
        out_specs=(anywhere,) * 3,
        scratch_shapes=[
            pltpu.VMEM((tokens, cb), BF16),
            pltpu.VMEM((tokens, cb), BF16),
            pltpu.VMEM((TAP_ROWS, cb), F32),
            pltpu.VMEM((groups, width), F32),
            pltpu.VMEM((half, channels // n), BF16),
            pltpu.VMEM((nb * cb, channels // nb), BF16),
            pltpu.VMEM((cb, tokens), BF16),
            pltpu.VMEM((cb, tokens), F32),
            pltpu.VMEM((cb, TAP_ROWS), F32),
            pltpu.VMEM((3, cb, tokens), F32),
            pltpu.VMEM((cb, tokens), F32),
            pltpu.VMEM((cb, tokens), F32),
            pltpu.VMEM((cb, tokens), BF16),
            pltpu.VMEM((cb, tokens), BF16),
            pltpu.VMEM((groups, width, 2 * width), BF16),
            pltpu.VMEM((nb * ntp * cb, tokens), BF16),
            pltpu.VMEM((n, cb, tokens), BF16),
            pltpu.VMEM((n, cb, tokens), BF16),
            pltpu.VMEM((cb, tokens), BF16),
            pltpu.VMEM((tokens, cb), BF16),
            pltpu.VMEM((cb, TAP_ROWS), F32),
            pltpu.VMEM((TAP_ROWS, cb), F32),
            pltpu.VMEM((groups, width), F32),
            dma((m,)),
            dma((m,)),
            dma((n,)),
            dma((n,)),
            dma((2,)),
            dma((2,)),
            dma((chunks, 2 * nb - 1)),
            dma((chunks, nb * ntp)),
            dma((ntp, nb * halves)),
            dma((n,)),
            dma((chunks,)),
            dma((chunks,)),
            dma((chunks, n)),
            dma((chunks, n)),
            dma((chunks, n)),
            dma((chunks, n)),
            dma((n,)),
            dma((n,)),
            dma((n,)),
            dma((n,)),
            dma((8,)),
        ],
        compiler_params=pltpu.CompilerParams(
            collective_id=0, has_side_effects=True, vmem_limit_bytes=52 * 1024 * 1024
        ),
        name="sections_backward",
    )(layer_inputs[0], out_grad, tap_rows, long_filters[0].astype(F32), out_weights[0])
    short_result = short_grad[: taps * 3].reshape(1, taps, 3, half)
    return (input_grad[None], short_result, long_grad[None])


def solution(mesh):
    in_specs = (
        P("pipe", ("seq", "tp"), None),
        P("seq", "tp"),
        P("pipe", None, None, "tp"),
        P("pipe", "tp", None),
        P("pipe", "tp", "seq"),
    )
    out_specs = (P("pipe", "seq", "tp"), P("pipe", None, None, "tp"), P("pipe", "tp", None))
    return jax.shard_map(
        per_device, mesh=mesh, in_specs=in_specs, out_specs=out_specs, check_vma=False
    )
```

```python
import functools

import jax
import jax.numpy as jnp
from jax import lax
from jax.experimental import pallas as pl
from jax.experimental.pallas import tpu as pltpu
from jax.sharding import PartitionSpec as P

MESH = pl.DeviceIdType.MESH
F32 = jnp.float32
BF16 = jnp.bfloat16
TAP_ROWS = 32


def remote(src, dst, send_sem, recv_sem, device):
    return pltpu.make_async_remote_copy(
        src_ref=src,
        dst_ref=dst,
        send_sem=send_sem,
        recv_sem=recv_sem,
        device_id=device,
        device_id_type=MESH,
    )


def aligned(index, size):
    return pl.ds(pl.multiple_of(index * size, size), size)


def kernel(
    dims,
    x_hbm,
    og_hbm,
    taps_hbm,
    filt_hbm,
    w_hbm,
    ig_out,
    short_out,
    long_out,
    xin,
    gin,
    taps_in,
    filt,
    w_vmem,
    w_swap,
    gate_sum,
    spill,
    xt,
    cols,
    feats,
    mixed,
    dkv,
    kv,
    dm,
    toep,
    gbuf,
    part,
    rs,
    ig,
    ot,
    short_cols,
    short_rows,
    long_rows,
    x_send,
    x_recv,
    og_send,
    og_recv,
    small_send,
    small_recv,
    ag_send,
    ag_recv,
    ws_send,
    ws_recv,
    z_send,
    z_recv,
    rs_send,
    rs_recv,
    ig_send,
    ig_recv,
    sg_send,
    sg_recv,
    lg_send,
    lg_recv,
    local_sem,
):
    sections, n, nb, ntp, tokens, cb, groups, width, taps, tw = dims
    halves = nb // ntp
    chip = ntp * cb
    m = n * ntp
    blocks = tokens // tw
    bands = tokens // width
    gw = cb // groups
    tl = tokens // n
    p, q, c = lax.axis_index("pipe"), lax.axis_index("seq"), lax.axis_index("tp")
    b = q * ntp + c
    half, slot = b // n, lax.rem(b, n)
    a, e = q // nb, lax.rem(q, nb)
    u, v = jnp.where(c == 0, a, e), jnp.where(c == 0, e, a)
    sibling = (p, q, 1 - c)
    owns = c == half
    last = p == sections - 1

    def place(block):
        return (p, block // ntp, lax.rem(block, ntp))

    barrier = pltpu.get_barrier_semaphore()
    for r in range(1, m):
        pl.semaphore_signal(
            barrier, inc=1, device_id=place(lax.rem(b + r, m)), device_id_type=MESH
        )

    @pl.when(p > 0)
    def _():
        pl.semaphore_signal(barrier, inc=1, device_id=(p - 1, q, c), device_id_type=MESH)

    @pl.when(p < sections - 1)
    def _():
        pl.semaphore_signal(barrier, inc=1, device_id=(p + 1, q, c), device_id_type=MESH)

    w_copy = pltpu.make_async_copy(w_hbm, w_vmem, local_sem.at[0])

    @pl.when(last)
    def _():
        w_copy.start()

    def swap_pieces():
        for i in range(halves):
            for j in range(nb):
                to, row = j, c * halves + i
                yield 0, i * nb + j, a * nb + to, row, row * nb + to, e
                to, row = c * halves + i, j
                yield 1, i * nb + j, to * nb + e, row, to * nb + row, a

    def swap_copies(piece):
        core, index, chip_to, row, owner, column = piece
        local = owner - c * (n // ntp)
        src = w_hbm.at[pl.ds(pl.multiple_of(local * chip + core * cb, cb), cb)]
        dst = w_swap.at[aligned(row, cb), aligned(column, chip)]
        send = ws_send.at[core, index]
        far = remote(src, dst, send, ws_recv.at[row * nb + column], (p, chip_to, core))
        near = pltpu.make_async_copy(src, dst, send)
        return jnp.logical_or(chip_to != q, core != c), far, near

    def swap_start():
        for piece in swap_pieces():
            away, far, near = swap_copies(piece)
            pl.when(away)(far.start)
            pl.when(jnp.logical_not(away))(near.start)

    def swap_sent():
        for piece in swap_pieces():
            away, far, near = swap_copies(piece)
            pl.when(away)(far.wait_send)

    def swap_arrived():
        for piece in swap_pieces():
            away, far, near = swap_copies(piece)
            pl.when(jnp.logical_not(away))(near.wait)
        for row in range(nb):
            owner = jnp.where(c == 0, row * nb + v, v * nb + row)
            for column in range(nb):
                away = jnp.logical_or(column != v, owner // (n // ntp) != c)
                far = remote(
                    w_hbm.at[pl.ds(0, cb)],
                    w_swap.at[pl.ds(row * cb, cb), pl.ds(column * chip, chip)],
                    ws_send.at[0, 0],
                    ws_recv.at[row * nb + column],
                    sibling,
                )
                pl.when(away)(far.wait_recv)

    x_rows = tokens // m
    x_local = pltpu.make_async_copy(
        x_hbm.at[:, aligned(b, cb)], xin.at[aligned(b, x_rows)], local_sem.at[1]
    )
    x_local.start()
    ends = (p > 0).astype(jnp.int32) + (p < sections - 1).astype(jnp.int32)
    pl.semaphore_wait(barrier, m - 1 + ends)

    def og_copy(j):
        block = c * n + j
        return block, remote(
            og_hbm.at[:, aligned(j, cb)],
            gin.at[aligned(q, tl)],
            og_send.at[j],
            og_recv.at[q],
            place(block),
        )

    @pl.when(last)
    def _():
        for j in range(n):
            block, copy = og_copy(j)

            @pl.when(block != b)
            def _():
                copy.start()

        @pl.when(owns)
        def _():
            own = pltpu.make_async_copy(
                og_hbm.at[:, aligned(slot, cb)], gin.at[aligned(q, tl)], local_sem.at[2]
            )
            own.start()
            own.wait()

    def x_copy(r):
        block = lax.rem(b + r, m)
        return remote(
            x_hbm.at[:, aligned(block, cb)],
            xin.at[aligned(b, x_rows)],
            x_send.at[r],
            x_recv.at[r],
            place(block),
        )

    for r in range(1, m):
        x_copy(r).start()

    other = lax.rem(q * ntp + 1 - c, n)
    taps_copy = remote(
        taps_hbm.at[:, aligned(other, cb)], taps_in, small_send.at[0], small_recv.at[0], sibling
    )
    filt_copy = remote(
        filt_hbm.at[aligned(other, groups)], filt, small_send.at[1], small_recv.at[1], sibling
    )

    @pl.when(owns)
    def _():
        taps_copy.start()
        filt_copy.start()
        taps_own = pltpu.make_async_copy(
            taps_hbm.at[:, aligned(slot, cb)], taps_in, local_sem.at[3]
        )
        filt_own = pltpu.make_async_copy(filt_hbm.at[aligned(slot, groups)], filt, local_sem.at[4])
        taps_own.start()
        filt_own.start()
        taps_own.wait()
        filt_own.wait()

    pl.when(jnp.logical_not(last))(swap_start)

    def grad_block(at, core, k):
        return gbuf.at[k, pl.ds(pl.multiple_of((at * ntp + core) * cb, cb), cb)]

    def gather_copy(k, index, at, device):
        return remote(
            grad_block(v, c, k),
            grad_block(at, c, k),
            ag_send.at[k, index],
            ag_recv.at[k, at * ntp + c],
            device,
        )

    def sib_copy(k):
        return gather_copy(k, 0, u, sibling)

    def gather_copies(k):
        copies = []
        for r in range(1, nb):
            to = lax.rem(e + r, nb)
            copies.append(gather_copy(k, r, e, (p, a * nb + to, 0)))
            to = lax.rem(a + r, nb)
            copies.append(gather_copy(k, nb - 1 + r, a, (p, to * nb + e, 1)))
        return copies

    def gather_wait(k, at, core):
        ref = grad_block(at, core, k)
        remote(ref, ref, ag_send.at[k, 0], ag_recv.at[k, at * ntp + core], sibling).wait_recv()

    def tokens_of(k):
        return pl.ds(pl.multiple_of(k * tw, tw), tw)

    def part_copy(j, k, block, source):
        return remote(
            part.at[k, j], rs.at[k, source], rs_send.at[k, j], rs_recv.at[k, source], place(block)
        )

    def part_block_last(j):
        return c * n + j

    def part_block(j):
        return jnp.where(c == 0, j * nb + v, v * nb + j) * ntp + c

    def dense(k, count, block_of, source, start, weight, grad):
        def one(step, carry):
            j = lax.rem(step + start, count)
            block = block_of(j)
            copy = part_copy(j, k, block, source)
            product = jnp.dot(
                weight[aligned(j, cb), :], grad[...], preferred_element_type=F32
            ).astype(BF16)

            @pl.when(block != b)
            def _():
                part[k, j] = product
                copy.start()

            @pl.when(block == b)
            def _():
                rs[k, source] = product

            return carry

        lax.fori_loop(0, count, one, 0)

    @pl.when(last)
    def _():
        for source in range(n):

            @pl.when(jnp.logical_or(source != q, jnp.logical_not(owns)))
            def _():
                remote(
                    og_hbm.at[:, pl.ds(0, cb)],
                    gin.at[pl.ds(source * tl, tl)],
                    og_send.at[0],
                    og_recv.at[source],
                    sibling,
                ).wait_recv()

        for k in range(blocks - 1, -1, -1):
            gbuf[k, aligned(v * ntp + c, cb), :] = (
                gin[pl.ds(k * tw, tw), :].astype(F32).T.astype(BF16)
            )
            sib_copy(k).start()
        w_copy.wait()

        def all_dense(step, carry):
            k = blocks - 1 - step
            gather_wait(k, v, 1 - c)
            dense(k, n, part_block_last, q, slot + 1, w_vmem, gbuf.at[k, aligned(v, chip)])
            return carry

        lax.fori_loop(0, blocks, all_dense, 0)

    x_local.wait()
    for r in range(1, m):
        source = lax.rem(b - r + m, m)
        remote(
            x_hbm.at[:, pl.ds(0, cb)],
            xin.at[aligned(source, x_rows)],
            x_send.at[r],
            x_recv.at[r],
            sibling,
        ).wait_recv()
    xt[:, pl.ds(0, width)] = jnp.zeros((cb, width), F32)
    for i in range(cb // 128):
        span = pl.ds(i * 128, 128)
        xt[span, pl.ds(width, tokens)] = xin[:, span].astype(F32).T
    dm[:, pl.ds(tokens, width)] = jnp.zeros((cb, width), BF16)
    spill[...] = jnp.zeros_like(spill)

    @pl.when(jnp.logical_not(owns))
    def _():
        taps_copy.wait_recv()
        filt_copy.wait_recv()

    cols[...] = taps_in[...].T
    lane = lax.broadcasted_iota(jnp.int32, (gw, tokens), 1)

    def later(value, by):
        if by == 0:
            return value
        return jnp.where(lane >= by, pltpu.roll(value, by, 1), 0.0)

    def stacked(value, count):
        return jnp.concatenate(
            [value[:, i * width : (i + 1) * width] for i in range(count)], axis=0
        )

    def windows(wide, count):
        return jnp.concatenate(
            [wide[:, i * width : (i + 2) * width] for i in range(count)], axis=0
        )

    def group_rows(g):
        return aligned(g, gw)

    def recompute(g, carry):
        rows = group_rows(g)
        source = xt[rows, pl.ds(width, tokens)]
        weight = cols[rows, :]
        running = [jnp.zeros((gw, tokens), F32)] * 3
        for j in range(taps):
            shifted = later(source, j)
            for f in range(3):
                running[f] = running[f] + weight[:, 3 * j + f : 3 * j + f + 1] * shifted
        for f in range(3):
            feats[f, rows, :] = running[f]
        product = (running[1] * running[2]).astype(BF16)
        kv[rows, :] = product
        tap_row = jnp.concatenate([filt[pl.ds(g, 1), :], jnp.zeros((1, width), F32)], axis=1)
        band = pltpu.roll(
            jnp.broadcast_to(tap_row, (width, 2 * width)), 0, 1, stride=1, stride_axis=0
        ).astype(BF16)
        toep[g] = band
        spread = jnp.dot(stacked(product, bands), band, preferred_element_type=F32)
        for i in range(bands):
            value = spread[i * gw : (i + 1) * gw, :width]
            if i > 0:
                value = value + spread[(i - 1) * gw : i * gw, width:]
            mixed[rows, pl.ds(i * width, width)] = value
        return carry

    lax.fori_loop(0, groups, recompute, 0, unroll=2)

    def z_copy(k):
        return remote(
            ig.at[k], grad_block(v, c, k), z_send.at[k], z_recv.at[k], (jnp.maximum(p - 1, 0), q, c)
        )

    def hand_on(k):
        z_copy(k).wait_recv()
        for copy in gather_copies(k):
            copy.start()
        sib_copy(k).start()

    @pl.when(jnp.logical_not(last))
    def _():
        hand_on(blocks - 1)
        swap_arrived()

    sub = tw // width
    block_lane = lax.broadcasted_iota(jnp.int32, (gw, tw), 1)

    def backward(k, g):
        rows = group_rows(g)
        span = tokens_of(k)
        gate = gate_sum[rows, :].astype(F32)
        mixed_grad = (gate * feats[0, rows, span]).astype(BF16)
        after = dm[rows, pl.ds(pl.multiple_of((k + 1) * tw, width), width)]
        dm[rows, span] = mixed_grad
        result = lax.dot_general(
            windows(jnp.concatenate([mixed_grad, after], axis=1), sub),
            toep[g],
            (((1,), (1,)), ((), ())),
            preferred_element_type=F32,
        )
        product_grad = jnp.concatenate([result[i * gw : (i + 1) * gw] for i in range(sub)], axis=1)
        dkv[rows, span] = product_grad
        query_grad = gate * mixed[rows, span]
        mixed[rows, span] = query_grad
        grads = (
            query_grad,
            product_grad * feats[2, rows, span],
            product_grad * feats[1, rows, span],
        )
        weight = cols[rows, :]
        total = gbuf[k, pl.ds(pl.multiple_of((v * ntp + c) * cb + g * gw, gw), gw), :].astype(F32)
        total = total + spill[rows, :]
        over = jnp.zeros((gw, tw), F32)
        for j in range(taps):
            term = weight[:, 3 * j : 3 * j + 1] * grads[0]
            for f in (1, 2):
                term = term + weight[:, 3 * j + f : 3 * j + f + 1] * grads[f]
            if j == 0:
                total = total + term
            else:
                moved = pltpu.roll(term, tw - j, 1)
                inside = block_lane < tw - j
                total = total + jnp.where(inside, moved, 0.0)
                over = over + jnp.where(inside, 0.0, moved)
        spill[rows, :] = over
        ig[k, rows, :] = total.astype(BF16)

    def each_group(body, unroll):
        def step(g, carry):
            body(g)
            return carry

        lax.fori_loop(0, groups, step, 0, unroll=unroll)

    def arrived(k, count, self_source, kept):
        for source in range(count):

            @pl.when(jnp.logical_or(source != self_source, jnp.logical_not(kept)))
            def _():
                remote(
                    part.at[k, 0],
                    rs.at[k, source],
                    rs_send.at[k, 0],
                    rs_recv.at[k, source],
                    sibling,
                ).wait_recv()

        def add(g):
            part_rows = group_rows(g)
            total = rs[k, 0, part_rows, :].astype(F32)
            for source in range(1, count):
                total = total + rs[k, source, part_rows, :].astype(F32)
            gate_sum[part_rows, :] = total.astype(BF16)

        each_group(add, 4)

    def give(src, dst, send_sem, recv_sem, target):
        copy = remote(src, dst, send_sem, recv_sem, (p, target, half))
        own = pltpu.make_async_copy(src, dst, send_sem)
        away = jnp.logical_or(target != q, jnp.logical_not(owns))

        def start():
            pl.when(away)(copy.start)
            pl.when(jnp.logical_not(away))(own.start)

        def sent():
            pl.when(away)(copy.wait_send)
            pl.when(jnp.logical_not(away))(own.wait)

        return start, sent

    def ig_give(target):
        return give(
            ot.at[pl.ds(pl.multiple_of(target * tl, tl), tl)],
            ig_out.at[:, aligned(slot, cb)],
            ig_send.at[target],
            ig_recv.at[slot],
            target,
        )

    def short_give(target):
        return give(
            short_rows,
            short_out.at[:, aligned(slot, cb)],
            sg_send.at[target],
            sg_recv.at[slot],
            target,
        )

    def long_give(target):
        return give(
            long_rows,
            long_out.at[aligned(slot, groups)],
            lg_send.at[target],
            lg_recv.at[slot],
            target,
        )

    def out_block(k):
        ot[tokens_of(k), :] = ig[k].astype(F32).T.astype(BF16)
        for i in range(tw // tl):
            ig_give(k * (tw // tl) + i)[0]()

    column = lax.broadcasted_iota(jnp.int32, (gw, TAP_ROWS), 1)
    low = lax.broadcasted_iota(jnp.int32, (8, 2 * width), 0)
    short_cols[...] = jnp.zeros_like(short_cols)

    def short_filters(k, g):
        rows = group_rows(g)
        span = tokens_of(k)
        source = xt[rows, pl.ds(pl.multiple_of(k * tw, width), tw + width)]
        product_grad = dkv[rows, span]
        grads = (
            mixed[rows, span],
            product_grad * feats[2, rows, span],
            product_grad * feats[1, rows, span],
        )
        sums = jnp.zeros((gw, TAP_ROWS), F32)
        for j in range(taps):
            shifted = (pltpu.roll(source, j, 1) if j else source)[:, width:]
            for f in range(3):
                total = jnp.sum(grads[f] * shifted, axis=1, keepdims=True)
                sums = jnp.where(column == 3 * j + f, total, sums)
        short_cols[rows, :] += sums

    def long_filters(g):
        rows = group_rows(g)
        lags = lax.dot_general(
            stacked(kv[rows, :], bands),
            windows(dm[rows, :], bands),
            (((0,), (0,)), ((), ())),
            preferred_element_type=F32,
        )
        size = width
        while size > 8:
            size //= 2
            lags = lags[:size] + pltpu.roll(lags[size:], 2 * width - size, 1)
        for bit in (4, 2, 1):
            lags = jnp.where((low & bit) != 0, pltpu.roll(lags, 2 * width - bit, 1), lags)
        long_rows[pl.ds(g, 1), :] = jnp.sum(lags, axis=0, keepdims=True)[:, :width]

    def section_step(step, carry):
        k = blocks - 1 - step

        @pl.when(last)
        def _():
            arrived(k, n, q, owns)

        @pl.when(jnp.logical_not(last))
        def _():
            for core in range(ntp):
                for r in range(nb):
                    if r:
                        gather_wait(k, lax.rem(v + r, nb), core)
            gather_wait(k, v, 1 - c)
            dense(k, nb, part_block, u, u + 1, w_swap, gbuf.at[k])

            @pl.when(k > 0)
            def _():
                hand_on(k - 1)

            arrived(k, nb, u, True)

        each_group(functools.partial(backward, k), 4)

        @pl.when(p > 0)
        def _():
            z_copy(k).start()

        @pl.when(p == 0)
        def _():
            out_block(k)
            each_group(functools.partial(short_filters, k), 2)

        return carry

    lax.fori_loop(0, blocks, section_step, 0)

    @pl.when(p > 0)
    def _():
        def finish(k, carry):
            out_block(k)
            each_group(functools.partial(short_filters, k), 2)
            return carry

        lax.fori_loop(0, blocks, finish, 0)

    each_group(long_filters, 2)
    short_rows[...] = short_cols[...].T
    for target in range(n):
        short_give(target)[0]()
        long_give(target)[0]()

    for j in range(n):

        @pl.when(c * n + j != b)
        def _():
            for src, dst, send, recv in (
                (ot.at[pl.ds(0, tl)], ig_out.at[:, pl.ds(j * cb, cb)], ig_send, ig_recv),
                (short_rows, short_out.at[:, pl.ds(j * cb, cb)], sg_send, sg_recv),
                (long_rows, long_out.at[pl.ds(j * groups, groups)], lg_send, lg_recv),
            ):
                remote(src, dst, send.at[0], recv.at[j], sibling).wait_recv()

    for target in range(n):
        short_give(target)[1]()
        long_give(target)[1]()
        ig_give(target)[1]()
    for r in range(1, m):
        x_copy(r).wait_send()

    @pl.when(owns)
    def _():
        taps_copy.wait_send()
        filt_copy.wait_send()

    @pl.when(last)
    def _():
        for j in range(n):
            block, copy = og_copy(j)

            @pl.when(block != b)
            def _():
                copy.wait_send()
                for k in range(blocks):
                    part_copy(j, k, block, q).wait_send()

    @pl.when(jnp.logical_not(last))
    def _():
        for j in range(nb):
            block = part_block(j)

            @pl.when(block != b)
            def _():
                for k in range(blocks):
                    part_copy(j, k, block, u).wait_send()

        swap_sent()
        for k in range(blocks):
            for copy in gather_copies(k):
                copy.wait_send()

    for k in range(blocks):
        sib_copy(k).wait_send()

        @pl.when(p > 0)
        def _():
            z_copy(k).wait_send()


def per_device(layer_inputs, out_grad, short_weights, long_filters, out_weights):
    sections, n, ntp = (lax.axis_size(a) for a in ("pipe", "seq", "tp"))
    m = n * ntp
    channels = layer_inputs.shape[2]
    tokens = layer_inputs.shape[1] * m
    cb = channels // m
    taps = short_weights.shape[1]
    width = long_filters.shape[2]
    groups = long_filters.shape[1] // n
    half = channels // ntp
    tw = width
    blocks = tokens // tw
    nb = max(d for d in range(1, n + 1) if d * d <= n)
    assert nb * nb == n and nb % ntp == 0
    halves = nb // ntp
    dims = (sections, n, nb, ntp, tokens, cb, groups, width, taps, tw)
    tap_rows = jnp.pad(
        short_weights.reshape(taps * 3, half).astype(F32), ((0, TAP_ROWS - taps * 3), (0, 0))
    )
    dma = pltpu.SemaphoreType.DMA
    anywhere = pl.BlockSpec(memory_space=pl.ANY)
    input_grad, short_grad, long_grad = pl.pallas_call(
        functools.partial(kernel, dims),
        out_shape=(
            jax.ShapeDtypeStruct((tokens // n, half), BF16),
            jax.ShapeDtypeStruct((TAP_ROWS, half), F32),
            jax.ShapeDtypeStruct((groups * n, width), F32),
        ),
        in_specs=[anywhere] * 5,
        out_specs=(anywhere,) * 3,
        scratch_shapes=[
            pltpu.VMEM((tokens, cb), BF16),
            pltpu.VMEM((tokens, cb), BF16),
            pltpu.VMEM((TAP_ROWS, cb), F32),
            pltpu.VMEM((groups, width), F32),
            pltpu.VMEM((half, channels // n), BF16),
            pltpu.VMEM((nb * cb, channels // nb), BF16),
            pltpu.VMEM((cb, tw), BF16),
            pltpu.VMEM((cb, tw), F32),
            pltpu.VMEM((cb, width + tokens), F32),
            pltpu.VMEM((cb, TAP_ROWS), F32),
            pltpu.VMEM((3, cb, tokens), F32),
            pltpu.VMEM((cb, tokens), F32),
            pltpu.VMEM((cb, tokens), F32),
            pltpu.VMEM((cb, tokens), BF16),
            pltpu.VMEM((cb, tokens + width), BF16),
            pltpu.VMEM((groups, width, 2 * width), BF16),
            pltpu.VMEM((blocks, nb * ntp * cb, tw), BF16),
            pltpu.VMEM((blocks, n, cb, tw), BF16),
            pltpu.VMEM((blocks, n, cb, tw), BF16),
            pltpu.VMEM((blocks, cb, tw), BF16),
            pltpu.VMEM((tokens, cb), BF16),
            pltpu.VMEM((cb, TAP_ROWS), F32),
            pltpu.VMEM((TAP_ROWS, cb), F32),
            pltpu.VMEM((groups, width), F32),
            dma((m,)),
            dma((m,)),
            dma((n,)),
            dma((n,)),
            dma((2,)),
            dma((2,)),
            dma((blocks, 2 * nb - 1)),
            dma((blocks, nb * ntp)),
            dma((ntp, nb * halves)),
            dma((n,)),
            dma((blocks,)),
            dma((blocks,)),
            dma((blocks, n)),
            dma((blocks, n)),
            dma((n,)),
            dma((n,)),
            dma((n,)),
            dma((n,)),
            dma((n,)),
            dma((n,)),
            dma((8,)),
        ],
        compiler_params=pltpu.CompilerParams(
            collective_id=0, has_side_effects=True, vmem_limit_bytes=52 * 1024 * 1024
        ),
        name="sections_backward",
    )(layer_inputs[0], out_grad, tap_rows, long_filters[0].astype(F32), out_weights[0])
    short_result = short_grad[: taps * 3].reshape(1, taps, 3, half)
    return (input_grad[None], short_result, long_grad[None])


def solution(mesh):
    in_specs = (
        P("pipe", ("seq", "tp"), None),
        P("seq", "tp"),
        P("pipe", None, None, "tp"),
        P("pipe", "tp", None),
        P("pipe", "tp", "seq"),
    )
    out_specs = (P("pipe", "seq", "tp"), P("pipe", None, None, "tp"), P("pipe", "tp", None))
    return jax.shard_map(
        per_device, mesh=mesh, in_specs=in_specs, out_specs=out_specs, check_vma=False
    )
```

```python
import functools

import jax
import jax.numpy as jnp
from jax import lax
from jax.experimental import pallas as pl
from jax.experimental.pallas import tpu as pltpu
from jax.sharding import PartitionSpec as P

MESH = pl.DeviceIdType.MESH
F32 = jnp.float32
BF16 = jnp.bfloat16
TAP_ROWS = 32


def remote(src, dst, send_sem, recv_sem, device):
    return pltpu.make_async_remote_copy(
        src_ref=src,
        dst_ref=dst,
        send_sem=send_sem,
        recv_sem=recv_sem,
        device_id=device,
        device_id_type=MESH,
    )


def aligned(index, size):
    return pl.ds(pl.multiple_of(index * size, size), size)


def kernel(
    dims,
    x_hbm,
    og_hbm,
    taps_hbm,
    filt_hbm,
    w_hbm,
    ig_out,
    short_out,
    long_out,
    xin,
    gin,
    taps_in,
    filt,
    w_vmem,
    w_swap,
    gate_sum,
    spill,
    xt,
    cols,
    feats,
    mixed,
    dkv,
    kv,
    dm,
    toep,
    gbuf,
    part,
    rs,
    ig,
    ot,
    short_cols,
    short_rows,
    long_rows,
    x_send,
    x_recv,
    og_send,
    og_recv,
    small_send,
    small_recv,
    ag_send,
    ag_recv,
    ws_send,
    ws_recv,
    z_send,
    z_recv,
    rs_send,
    rs_recv,
    ig_send,
    ig_recv,
    sg_send,
    sg_recv,
    lg_send,
    lg_recv,
    local_sem,
):
    sections, n, nb, ntp, tokens, cb, groups, width, taps, tw = dims
    halves = nb // ntp
    chip = ntp * cb
    m = n * ntp
    blocks = tokens // tw
    bands = tokens // width
    gw = cb // groups
    tl = tokens // n
    p, q, c = lax.axis_index("pipe"), lax.axis_index("seq"), lax.axis_index("tp")
    b = q * ntp + c
    half, slot = b // n, lax.rem(b, n)
    a, e = q // nb, lax.rem(q, nb)
    u, v = jnp.where(c == 0, a, e), jnp.where(c == 0, e, a)
    sibling = (p, q, 1 - c)
    owns = c == half
    last = p == sections - 1

    def place(block):
        return (p, block // ntp, lax.rem(block, ntp))

    barrier = pltpu.get_barrier_semaphore()
    for r in range(1, m):
        pl.semaphore_signal(
            barrier, inc=1, device_id=place(lax.rem(b + r, m)), device_id_type=MESH
        )

    @pl.when(p > 0)
    def _():
        pl.semaphore_signal(barrier, inc=1, device_id=(p - 1, q, c), device_id_type=MESH)

    @pl.when(p < sections - 1)
    def _():
        pl.semaphore_signal(barrier, inc=1, device_id=(p + 1, q, c), device_id_type=MESH)

    w_copy = pltpu.make_async_copy(w_hbm, w_vmem, local_sem.at[0])

    @pl.when(last)
    def _():
        w_copy.start()

    def swap_pieces():
        for i in range(halves):
            for j in range(nb):
                to, row = j, c * halves + i
                yield 0, i * nb + j, a * nb + to, row, row * nb + to, e
                to, row = c * halves + i, j
                yield 1, i * nb + j, to * nb + e, row, to * nb + row, a

    def swap_copies(piece):
        core, index, chip_to, row, owner, column = piece
        local = owner - c * (n // ntp)
        src = w_hbm.at[pl.ds(pl.multiple_of(local * chip + core * cb, cb), cb)]
        dst = w_swap.at[aligned(row, cb), aligned(column, chip)]
        send = ws_send.at[core, index]
        far = remote(src, dst, send, ws_recv.at[row * nb + column], (p, chip_to, core))
        near = pltpu.make_async_copy(src, dst, send)
        return jnp.logical_or(chip_to != q, core != c), far, near

    def swap_start():
        for piece in swap_pieces():
            away, far, near = swap_copies(piece)
            pl.when(away)(far.start)
            pl.when(jnp.logical_not(away))(near.start)

    def swap_sent():
        for piece in swap_pieces():
            away, far, near = swap_copies(piece)
            pl.when(away)(far.wait_send)

    def swap_arrived():
        for piece in swap_pieces():
            away, far, near = swap_copies(piece)
            pl.when(jnp.logical_not(away))(near.wait)
        for row in range(nb):
            owner = jnp.where(c == 0, row * nb + v, v * nb + row)
            for column in range(nb):
                away = jnp.logical_or(column != v, owner // (n // ntp) != c)
                far = remote(
                    w_hbm.at[pl.ds(0, cb)],
                    w_swap.at[pl.ds(row * cb, cb), pl.ds(column * chip, chip)],
                    ws_send.at[0, 0],
                    ws_recv.at[row * nb + column],
                    sibling,
                )
                pl.when(away)(far.wait_recv)

    x_rows = tokens // m
    x_local = pltpu.make_async_copy(
        x_hbm.at[:, aligned(b, cb)], xin.at[aligned(b, x_rows)], local_sem.at[1]
    )
    x_local.start()
    ends = (p > 0).astype(jnp.int32) + (p < sections - 1).astype(jnp.int32)
    pl.semaphore_wait(barrier, m - 1 + ends)

    def og_copy(j):
        block = c * n + j
        return block, remote(
            og_hbm.at[:, aligned(j, cb)],
            gin.at[aligned(q, tl)],
            og_send.at[j],
            og_recv.at[q],
            place(block),
        )

    @pl.when(last)
    def _():
        for j in range(n):
            block, copy = og_copy(j)

            @pl.when(block != b)
            def _():
                copy.start()

        @pl.when(owns)
        def _():
            own = pltpu.make_async_copy(
                og_hbm.at[:, aligned(slot, cb)], gin.at[aligned(q, tl)], local_sem.at[2]
            )
            own.start()
            own.wait()

    def x_copy(r):
        block = lax.rem(b + r, m)
        return remote(
            x_hbm.at[:, aligned(block, cb)],
            xin.at[aligned(b, x_rows)],
            x_send.at[r],
            x_recv.at[r],
            place(block),
        )

    for r in range(1, m):
        x_copy(r).start()

    other = lax.rem(q * ntp + 1 - c, n)
    taps_copy = remote(
        taps_hbm.at[:, aligned(other, cb)], taps_in, small_send.at[0], small_recv.at[0], sibling
    )
    filt_copy = remote(
        filt_hbm.at[aligned(other, groups)], filt, small_send.at[1], small_recv.at[1], sibling
    )

    @pl.when(owns)
    def _():
        taps_copy.start()
        filt_copy.start()
        taps_own = pltpu.make_async_copy(
            taps_hbm.at[:, aligned(slot, cb)], taps_in, local_sem.at[3]
        )
        filt_own = pltpu.make_async_copy(filt_hbm.at[aligned(slot, groups)], filt, local_sem.at[4])
        taps_own.start()
        filt_own.start()
        taps_own.wait()
        filt_own.wait()

    pl.when(jnp.logical_not(last))(swap_start)

    def grad_block(at, core, k):
        return gbuf.at[k, pl.ds(pl.multiple_of((at * ntp + core) * cb, cb), cb)]

    def gather_copy(k, index, at, device):
        return remote(
            grad_block(v, c, k),
            grad_block(at, c, k),
            ag_send.at[k, index],
            ag_recv.at[k, at * ntp + c],
            device,
        )

    def sib_copy(k):
        return gather_copy(k, 0, u, sibling)

    def gather_copies(k):
        copies = []
        for r in range(1, nb):
            to = lax.rem(e + r, nb)
            copies.append(gather_copy(k, r, e, (p, a * nb + to, 0)))
            to = lax.rem(a + r, nb)
            copies.append(gather_copy(k, nb - 1 + r, a, (p, to * nb + e, 1)))
        return copies

    def gather_wait(k, at, core):
        ref = grad_block(at, core, k)
        remote(ref, ref, ag_send.at[k, 0], ag_recv.at[k, at * ntp + core], sibling).wait_recv()

    def tokens_of(k):
        return pl.ds(pl.multiple_of(k * tw, tw), tw)

    def part_copy(j, k, block, source):
        return remote(
            part.at[k, j], rs.at[k, source], rs_send.at[k, j], rs_recv.at[k, source], place(block)
        )

    def part_block_last(j):
        return c * n + j

    def part_block(j):
        return jnp.where(c == 0, j * nb + v, v * nb + j) * ntp + c

    def dense(k, count, block_of, source, start, weight, grad):
        def one(step, carry):
            j = lax.rem(step + start, count)
            block = block_of(j)
            copy = part_copy(j, k, block, source)
            product = jnp.dot(
                weight[aligned(j, cb), :], grad[...], preferred_element_type=F32
            ).astype(BF16)

            @pl.when(block != b)
            def _():
                part[k, j] = product
                copy.start()

            @pl.when(block == b)
            def _():
                rs[k, source] = product

            return carry

        lax.fori_loop(0, count, one, 0)

    @pl.when(last)
    def _():
        for source in range(n):

            @pl.when(jnp.logical_or(source != q, jnp.logical_not(owns)))
            def _():
                remote(
                    og_hbm.at[:, pl.ds(0, cb)],
                    gin.at[pl.ds(source * tl, tl)],
                    og_send.at[0],
                    og_recv.at[source],
                    sibling,
                ).wait_recv()

        for k in range(blocks - 1, -1, -1):
            gbuf[k, aligned(v * ntp + c, cb), :] = (
                gin[pl.ds(k * tw, tw), :].astype(F32).T.astype(BF16)
            )
            sib_copy(k).start()
        w_copy.wait()

        def all_dense(step, carry):
            k = blocks - 1 - step
            gather_wait(k, v, 1 - c)
            dense(k, n, part_block_last, q, slot + 1, w_vmem, gbuf.at[k, aligned(v, chip)])
            return carry

        lax.fori_loop(0, blocks, all_dense, 0)

    x_local.wait()
    for r in range(1, m):
        source = lax.rem(b - r + m, m)
        remote(
            x_hbm.at[:, pl.ds(0, cb)],
            xin.at[aligned(source, x_rows)],
            x_send.at[r],
            x_recv.at[r],
            sibling,
        ).wait_recv()
    xt[:, pl.ds(0, width)] = jnp.zeros((cb, width), F32)
    for i in range(cb // 128):
        span = pl.ds(i * 128, 128)
        xt[span, pl.ds(width, tokens)] = xin[:, span].astype(F32).T
    dm[:, pl.ds(tokens, width)] = jnp.zeros((cb, width), BF16)
    spill[...] = jnp.zeros_like(spill)

    @pl.when(jnp.logical_not(owns))
    def _():
        taps_copy.wait_recv()
        filt_copy.wait_recv()

    cols[...] = taps_in[...].T
    lane = lax.broadcasted_iota(jnp.int32, (gw, tokens), 1)

    def later(value, by):
        if by == 0:
            return value
        return jnp.where(lane >= by, pltpu.roll(value, by, 1), 0.0)

    def stacked(value, count):
        return jnp.concatenate(
            [value[:, i * width : (i + 1) * width] for i in range(count)], axis=0
        )

    def windows(wide, count):
        return jnp.concatenate(
            [wide[:, i * width : (i + 2) * width] for i in range(count)], axis=0
        )

    def group_rows(g):
        return aligned(g, gw)

    def recompute(g, carry):
        rows = group_rows(g)
        source = xt[rows, pl.ds(width, tokens)]
        weight = cols[rows, :]
        running = [jnp.zeros((gw, tokens), F32)] * 3
        for j in range(taps):
            shifted = later(source, j)
            for f in range(3):
                running[f] = running[f] + weight[:, 3 * j + f : 3 * j + f + 1] * shifted
        for f in range(3):
            feats[f, rows, :] = running[f]
        product = (running[1] * running[2]).astype(BF16)
        kv[rows, :] = product
        tap_row = jnp.concatenate([filt[pl.ds(g, 1), :], jnp.zeros((1, width), F32)], axis=1)
        band = pltpu.roll(
            jnp.broadcast_to(tap_row, (width, 2 * width)), 0, 1, stride=1, stride_axis=0
        ).astype(BF16)
        toep[g] = band
        spread = jnp.dot(stacked(product, bands), band, preferred_element_type=F32)
        for i in range(bands):
            value = spread[i * gw : (i + 1) * gw, :width]
            if i > 0:
                value = value + spread[(i - 1) * gw : i * gw, width:]
            mixed[rows, pl.ds(i * width, width)] = value
        return carry

    lax.fori_loop(0, groups, recompute, 0, unroll=2)

    def z_copy(k):
        return remote(
            ig.at[k], grad_block(v, c, k), z_send.at[k], z_recv.at[k], (jnp.maximum(p - 1, 0), q, c)
        )

    def hand_on(k):
        z_copy(k).wait_recv()
        for copy in gather_copies(k):
            copy.start()
        sib_copy(k).start()

    @pl.when(jnp.logical_not(last))
    def _():
        hand_on(blocks - 1)
        swap_arrived()

    sub = tw // width
    batch = next(d for d in (4, 2, 1) if groups % d == 0)
    bulk = batch * gw
    block_lane = lax.broadcasted_iota(jnp.int32, (bulk, tw), 1)

    def backward(k, s):
        rows = aligned(s, bulk)
        span = tokens_of(k)
        gate = gate_sum[rows, :].astype(F32)
        mixed_grad = (gate * feats[0, rows, span]).astype(BF16)
        after = dm[rows, pl.ds(pl.multiple_of((k + 1) * tw, width), width)]
        wide = jnp.concatenate([mixed_grad, after], axis=1)
        pieces = []
        for i in range(batch):
            result = lax.dot_general(
                windows(wide[i * gw : (i + 1) * gw], sub),
                toep[s * batch + i],
                (((1,), (1,)), ((), ())),
                preferred_element_type=F32,
            )
            pieces.append(
                jnp.concatenate([result[r * gw : (r + 1) * gw] for r in range(sub)], axis=1)
            )
        product_grad = jnp.concatenate(pieces, axis=0)
        query_grad = gate * mixed[rows, span]
        grads = (
            query_grad,
            product_grad * feats[2, rows, span],
            product_grad * feats[1, rows, span],
        )
        weight = cols[rows, :]
        own = pl.ds(pl.multiple_of((v * ntp + c) * cb + s * bulk, bulk), bulk)
        total = gbuf[k, own, :].astype(F32)
        total = total + spill[rows, :]
        over = jnp.zeros((bulk, tw), F32)
        for j in range(taps):
            term = weight[:, 3 * j : 3 * j + 1] * grads[0]
            for f in (1, 2):
                term = term + weight[:, 3 * j + f : 3 * j + f + 1] * grads[f]
            if j == 0:
                total = total + term
            else:
                moved = pltpu.roll(term, tw - j, 1)
                inside = block_lane < tw - j
                total = total + jnp.where(inside, moved, 0.0)
                over = over + jnp.where(inside, 0.0, moved)
        dm[rows, span] = mixed_grad
        dkv[rows, span] = product_grad
        mixed[rows, span] = query_grad
        spill[rows, :] = over
        ig[k, rows, :] = total.astype(BF16)

    def each(count, body, unroll):
        def step(g, carry):
            body(g)
            return carry

        lax.fori_loop(0, count, step, 0, unroll=unroll)

    def arrived(k, count, self_source, kept):
        for source in range(count):

            @pl.when(jnp.logical_or(source != self_source, jnp.logical_not(kept)))
            def _():
                remote(
                    part.at[k, 0],
                    rs.at[k, source],
                    rs_send.at[k, 0],
                    rs_recv.at[k, source],
                    sibling,
                ).wait_recv()

        def add(g):
            part_rows = aligned(g, bulk)
            total = rs[k, 0, part_rows, :].astype(F32)
            for source in range(1, count):
                total = total + rs[k, source, part_rows, :].astype(F32)
            gate_sum[part_rows, :] = total.astype(BF16)

        each(groups // batch, add, 2)

    def give(src, dst, send_sem, recv_sem, target):
        copy = remote(src, dst, send_sem, recv_sem, (p, target, half))
        own = pltpu.make_async_copy(src, dst, send_sem)
        away = jnp.logical_or(target != q, jnp.logical_not(owns))

        def start():
            pl.when(away)(copy.start)
            pl.when(jnp.logical_not(away))(own.start)

        def sent():
            pl.when(away)(copy.wait_send)
            pl.when(jnp.logical_not(away))(own.wait)

        return start, sent

    def ig_give(target):
        return give(
            ot.at[pl.ds(pl.multiple_of(target * tl, tl), tl)],
            ig_out.at[:, aligned(slot, cb)],
            ig_send.at[target],
            ig_recv.at[slot],
            target,
        )

    def short_give(target):
        return give(
            short_rows,
            short_out.at[:, aligned(slot, cb)],
            sg_send.at[target],
            sg_recv.at[slot],
            target,
        )

    def long_give(target):
        return give(
            long_rows,
            long_out.at[aligned(slot, groups)],
            lg_send.at[target],
            lg_recv.at[slot],
            target,
        )

    def out_block(k):
        ot[tokens_of(k), :] = ig[k].astype(F32).T.astype(BF16)
        for i in range(tw // tl):
            ig_give(k * (tw // tl) + i)[0]()

    column = lax.broadcasted_iota(jnp.int32, (gw, TAP_ROWS), 1)
    low = lax.broadcasted_iota(jnp.int32, (8, 2 * width), 0)

    def filters(g):
        rows = group_rows(g)
        source = xt[rows, pl.ds(width, tokens)]
        product_grad = dkv[rows, :]
        grads = (
            mixed[rows, :],
            product_grad * feats[2, rows, :],
            product_grad * feats[1, rows, :],
        )
        sums = jnp.zeros((gw, TAP_ROWS), F32)
        for j in range(taps):
            shifted = later(source, j)
            for f in range(3):
                total = jnp.sum(grads[f] * shifted, axis=1, keepdims=True)
                sums = jnp.where(column == 3 * j + f, total, sums)
        short_cols[rows, :] = sums
        lags = lax.dot_general(
            stacked(kv[rows, :], bands),
            windows(dm[rows, :], bands),
            (((0,), (0,)), ((), ())),
            preferred_element_type=F32,
        )
        size = width
        while size > 8:
            size //= 2
            lags = lags[:size] + pltpu.roll(lags[size:], 2 * width - size, 1)
        for bit in (4, 2, 1):
            lags = jnp.where((low & bit) != 0, pltpu.roll(lags, 2 * width - bit, 1), lags)
        long_rows[pl.ds(g, 1), :] = jnp.sum(lags, axis=0, keepdims=True)[:, :width]

    def section_step(step, carry):
        k = blocks - 1 - step

        @pl.when(last)
        def _():
            arrived(k, n, q, owns)

        @pl.when(jnp.logical_not(last))
        def _():
            for core in range(ntp):
                for r in range(nb):
                    if r:
                        gather_wait(k, lax.rem(v + r, nb), core)
            gather_wait(k, v, 1 - c)
            dense(k, nb, part_block, u, u + 1, w_swap, gbuf.at[k])

            @pl.when(k > 0)
            def _():
                hand_on(k - 1)

            arrived(k, nb, u, True)

        each(groups // batch, functools.partial(backward, k), 2)

        @pl.when(p > 0)
        def _():
            z_copy(k).start()

        @pl.when(p == 0)
        def _():
            out_block(k)

        return carry

    lax.fori_loop(0, blocks, section_step, 0)

    @pl.when(p > 0)
    def _():
        def finish(k, carry):
            out_block(k)
            return carry

        lax.fori_loop(0, blocks, finish, 0)

    each(groups, filters, 2)
    short_rows[...] = short_cols[...].T
    for target in range(n):
        short_give(target)[0]()
        long_give(target)[0]()

    for j in range(n):

        @pl.when(c * n + j != b)
        def _():
            for src, dst, send, recv in (
                (ot.at[pl.ds(0, tl)], ig_out.at[:, pl.ds(j * cb, cb)], ig_send, ig_recv),
                (short_rows, short_out.at[:, pl.ds(j * cb, cb)], sg_send, sg_recv),
                (long_rows, long_out.at[pl.ds(j * groups, groups)], lg_send, lg_recv),
            ):
                remote(src, dst, send.at[0], recv.at[j], sibling).wait_recv()

    for target in range(n):
        short_give(target)[1]()
        long_give(target)[1]()
        ig_give(target)[1]()
    for r in range(1, m):
        x_copy(r).wait_send()

    @pl.when(owns)
    def _():
        taps_copy.wait_send()
        filt_copy.wait_send()

    @pl.when(last)
    def _():
        for j in range(n):
            block, copy = og_copy(j)

            @pl.when(block != b)
            def _():
                copy.wait_send()
                for k in range(blocks):
                    part_copy(j, k, block, q).wait_send()

    @pl.when(jnp.logical_not(last))
    def _():
        for j in range(nb):
            block = part_block(j)

            @pl.when(block != b)
            def _():
                for k in range(blocks):
                    part_copy(j, k, block, u).wait_send()

        swap_sent()
        for k in range(blocks):
            for copy in gather_copies(k):
                copy.wait_send()

    for k in range(blocks):
        sib_copy(k).wait_send()

        @pl.when(p > 0)
        def _():
            z_copy(k).wait_send()


def per_device(layer_inputs, out_grad, short_weights, long_filters, out_weights):
    sections, n, ntp = (lax.axis_size(a) for a in ("pipe", "seq", "tp"))
    m = n * ntp
    channels = layer_inputs.shape[2]
    tokens = layer_inputs.shape[1] * m
    cb = channels // m
    taps = short_weights.shape[1]
    width = long_filters.shape[2]
    groups = long_filters.shape[1] // n
    half = channels // ntp
    tw = width
    blocks = tokens // tw
    nb = max(d for d in range(1, n + 1) if d * d <= n)
    assert nb * nb == n and nb % ntp == 0
    halves = nb // ntp
    dims = (sections, n, nb, ntp, tokens, cb, groups, width, taps, tw)
    tap_rows = jnp.pad(
        short_weights.reshape(taps * 3, half).astype(F32), ((0, TAP_ROWS - taps * 3), (0, 0))
    )
    dma = pltpu.SemaphoreType.DMA
    anywhere = pl.BlockSpec(memory_space=pl.ANY)
    input_grad, short_grad, long_grad = pl.pallas_call(
        functools.partial(kernel, dims),
        out_shape=(
            jax.ShapeDtypeStruct((tokens // n, half), BF16),
            jax.ShapeDtypeStruct((TAP_ROWS, half), F32),
            jax.ShapeDtypeStruct((groups * n, width), F32),
        ),
        in_specs=[anywhere] * 5,
        out_specs=(anywhere,) * 3,
        scratch_shapes=[
            pltpu.VMEM((tokens, cb), BF16),
            pltpu.VMEM((tokens, cb), BF16),
            pltpu.VMEM((TAP_ROWS, cb), F32),
            pltpu.VMEM((groups, width), F32),
            pltpu.VMEM((half, channels // n), BF16),
            pltpu.VMEM((nb * cb, channels // nb), BF16),
            pltpu.VMEM((cb, tw), BF16),
            pltpu.VMEM((cb, tw), F32),
            pltpu.VMEM((cb, width + tokens), F32),
            pltpu.VMEM((cb, TAP_ROWS), F32),
            pltpu.VMEM((3, cb, tokens), F32),
            pltpu.VMEM((cb, tokens), F32),
            pltpu.VMEM((cb, tokens), F32),
            pltpu.VMEM((cb, tokens), BF16),
            pltpu.VMEM((cb, tokens + width), BF16),
            pltpu.VMEM((groups, width, 2 * width), BF16),
            pltpu.VMEM((blocks, nb * ntp * cb, tw), BF16),
            pltpu.VMEM((blocks, n, cb, tw), BF16),
            pltpu.VMEM((blocks, n, cb, tw), BF16),
            pltpu.VMEM((blocks, cb, tw), BF16),
            pltpu.VMEM((tokens, cb), BF16),
            pltpu.VMEM((cb, TAP_ROWS), F32),
            pltpu.VMEM((TAP_ROWS, cb), F32),
            pltpu.VMEM((groups, width), F32),
            dma((m,)),
            dma((m,)),
            dma((n,)),
            dma((n,)),
            dma((2,)),
            dma((2,)),
            dma((blocks, 2 * nb - 1)),
            dma((blocks, nb * ntp)),
            dma((ntp, nb * halves)),
            dma((n,)),
            dma((blocks,)),
            dma((blocks,)),
            dma((blocks, n)),
            dma((blocks, n)),
            dma((n,)),
            dma((n,)),
            dma((n,)),
            dma((n,)),
            dma((n,)),
            dma((n,)),
            dma((8,)),
        ],
        compiler_params=pltpu.CompilerParams(
            collective_id=0, has_side_effects=True, vmem_limit_bytes=52 * 1024 * 1024
        ),
        name="sections_backward",
    )(layer_inputs[0], out_grad, tap_rows, long_filters[0].astype(F32), out_weights[0])
    short_result = short_grad[: taps * 3].reshape(1, taps, 3, half)
    return (input_grad[None], short_result, long_grad[None])


def solution(mesh):
    in_specs = (
        P("pipe", ("seq", "tp"), None),
        P("seq", "tp"),
        P("pipe", None, None, "tp"),
        P("pipe", "tp", None),
        P("pipe", "tp", "seq"),
    )
    out_specs = (P("pipe", "seq", "tp"), P("pipe", None, None, "tp"), P("pipe", "tp", None))
    return jax.shard_map(
        per_device, mesh=mesh, in_specs=in_specs, out_specs=out_specs, check_vma=False
    )
```

```python
import functools

import jax
import jax.numpy as jnp
from jax import lax
from jax.experimental import pallas as pl
from jax.experimental.pallas import tpu as pltpu
from jax.sharding import PartitionSpec as P

MESH = pl.DeviceIdType.MESH
F32 = jnp.float32
BF16 = jnp.bfloat16
TAP_ROWS = 32


def remote(src, dst, send_sem, recv_sem, device):
    return pltpu.make_async_remote_copy(
        src_ref=src,
        dst_ref=dst,
        send_sem=send_sem,
        recv_sem=recv_sem,
        device_id=device,
        device_id_type=MESH,
    )


def aligned(index, size):
    return pl.ds(pl.multiple_of(index * size, size), size)


def kernel(
    dims,
    x_hbm,
    og_hbm,
    taps_hbm,
    filt_hbm,
    w_hbm,
    ig_out,
    short_out,
    long_out,
    xin,
    gin,
    taps_in,
    filt,
    w_vmem,
    w_swap,
    gate_sum,
    xt,
    cols,
    feats,
    mixed,
    dkv,
    kv,
    dm,
    toep,
    gbuf,
    part,
    rs,
    ig,
    ot,
    short_cols,
    short_rows,
    long_rows,
    x_send,
    x_recv,
    og_send,
    og_recv,
    small_send,
    small_recv,
    ag_send,
    ag_recv,
    ws_send,
    ws_recv,
    z_send,
    z_recv,
    rs_send,
    rs_recv,
    ig_send,
    ig_recv,
    sg_send,
    sg_recv,
    lg_send,
    lg_recv,
    local_sem,
):
    sections, n, nb, ntp, tokens, cb, groups, width, taps, chunk = dims
    halves = nb // ntp
    chip = ntp * cb
    m = n * ntp
    chunks = cb // chunk
    blocks = tokens // width
    gw = cb // groups
    tl = tokens // n
    p, q, c = lax.axis_index("pipe"), lax.axis_index("seq"), lax.axis_index("tp")
    b = q * ntp + c
    half, slot = b // n, lax.rem(b, n)
    a, e = q // nb, lax.rem(q, nb)
    u, v = jnp.where(c == 0, a, e), jnp.where(c == 0, e, a)
    sibling = (p, q, 1 - c)
    owns = c == half
    last = p == sections - 1

    def place(block):
        return (p, block // ntp, lax.rem(block, ntp))

    barrier = pltpu.get_barrier_semaphore()
    for r in range(1, m):
        pl.semaphore_signal(
            barrier, inc=1, device_id=place(lax.rem(b + r, m)), device_id_type=MESH
        )

    @pl.when(p > 0)
    def _():
        pl.semaphore_signal(barrier, inc=1, device_id=(p - 1, q, c), device_id_type=MESH)

    @pl.when(p < sections - 1)
    def _():
        pl.semaphore_signal(barrier, inc=1, device_id=(p + 1, q, c), device_id_type=MESH)

    w_copy = pltpu.make_async_copy(w_hbm, w_vmem, local_sem.at[0])

    @pl.when(last)
    def _():
        w_copy.start()

    def swap_pieces():
        for i in range(halves):
            for j in range(nb):
                to, row = j, c * halves + i
                yield 0, i * nb + j, a * nb + to, row, row * nb + to, e
                to, row = c * halves + i, j
                yield 1, i * nb + j, to * nb + e, row, to * nb + row, a

    def swap_copies(piece):
        core, index, chip_to, row, owner, column = piece
        local = owner - c * (n // ntp)
        src = w_hbm.at[pl.ds(pl.multiple_of(local * chip + core * cb, cb), cb)]
        dst = w_swap.at[aligned(row, cb), aligned(column, chip)]
        send = ws_send.at[core, index]
        far = remote(src, dst, send, ws_recv.at[row * nb + column], (p, chip_to, core))
        near = pltpu.make_async_copy(src, dst, send)
        return jnp.logical_or(chip_to != q, core != c), far, near

    def swap_start():
        for piece in swap_pieces():
            away, far, near = swap_copies(piece)
            pl.when(away)(far.start)
            pl.when(jnp.logical_not(away))(near.start)

    def swap_sent():
        for piece in swap_pieces():
            away, far, near = swap_copies(piece)
            pl.when(away)(far.wait_send)

    def swap_arrived():
        for piece in swap_pieces():
            away, far, near = swap_copies(piece)
            pl.when(jnp.logical_not(away))(near.wait)
        for row in range(nb):
            owner = jnp.where(c == 0, row * nb + v, v * nb + row)
            for column in range(nb):
                away = jnp.logical_or(column != v, owner // (n // ntp) != c)
                far = remote(
                    w_hbm.at[pl.ds(0, cb)],
                    w_swap.at[pl.ds(row * cb, cb), pl.ds(column * chip, chip)],
                    ws_send.at[0, 0],
                    ws_recv.at[row * nb + column],
                    sibling,
                )
                pl.when(away)(far.wait_recv)

    x_rows = tokens // m
    x_local = pltpu.make_async_copy(
        x_hbm.at[:, aligned(b, cb)], xin.at[aligned(b, x_rows)], local_sem.at[1]
    )
    x_local.start()
    ends = (p > 0).astype(jnp.int32) + (p < sections - 1).astype(jnp.int32)
    pl.semaphore_wait(barrier, m - 1 + ends)

    def og_copy(j):
        block = c * n + j
        return block, remote(
            og_hbm.at[:, aligned(j, cb)],
            gin.at[aligned(q, tl)],
            og_send.at[j],
            og_recv.at[q],
            place(block),
        )

    @pl.when(last)
    def _():
        for j in range(n):
            block, copy = og_copy(j)

            @pl.when(block != b)
            def _():
                copy.start()

        @pl.when(owns)
        def _():
            own = pltpu.make_async_copy(
                og_hbm.at[:, aligned(slot, cb)], gin.at[aligned(q, tl)], local_sem.at[2]
            )
            own.start()
            own.wait()

    def x_copy(r):
        block = lax.rem(b + r, m)
        return remote(
            x_hbm.at[:, aligned(block, cb)],
            xin.at[aligned(b, x_rows)],
            x_send.at[r],
            x_recv.at[r],
            place(block),
        )

    for r in range(1, m):
        x_copy(r).start()

    other = lax.rem(q * ntp + 1 - c, n)
    taps_copy = remote(
        taps_hbm.at[:, aligned(other, cb)], taps_in, small_send.at[0], small_recv.at[0], sibling
    )
    filt_copy = remote(
        filt_hbm.at[aligned(other, groups)], filt, small_send.at[1], small_recv.at[1], sibling
    )

    @pl.when(owns)
    def _():
        taps_copy.start()
        filt_copy.start()
        taps_own = pltpu.make_async_copy(
            taps_hbm.at[:, aligned(slot, cb)], taps_in, local_sem.at[3]
        )
        filt_own = pltpu.make_async_copy(filt_hbm.at[aligned(slot, groups)], filt, local_sem.at[4])
        taps_own.start()
        filt_own.start()
        taps_own.wait()
        filt_own.wait()

    pl.when(jnp.logical_not(last))(swap_start)

    def grad_rows(at, core, k):
        return pl.ds(pl.multiple_of((at * ntp + core) * cb + k * chunk, chunk), chunk)

    def gather_copy(k, index, at, device):
        return remote(
            gbuf.at[grad_rows(v, c, k)],
            gbuf.at[grad_rows(at, c, k)],
            ag_send.at[k, index],
            ag_recv.at[k, at * ntp + c],
            device,
        )

    def sib_copy(k):
        return gather_copy(k, 0, u, sibling)

    def gather_copies(k):
        copies = []
        for r in range(1, nb):
            to = lax.rem(e + r, nb)
            copies.append(gather_copy(k, r, e, (p, a * nb + to, 0)))
            to = lax.rem(a + r, nb)
            copies.append(gather_copy(k, nb - 1 + r, a, (p, to * nb + e, 1)))
        return copies

    def gather_wait(k, at, core):
        ref = gbuf.at[grad_rows(at, core, k)]
        remote(ref, ref, ag_send.at[k, 0], ag_recv.at[k, at * ntp + core], sibling).wait_recv()

    def span_of(k):
        return pl.ds(pl.multiple_of(k * chunk, chunk), chunk)

    def part_copy(j, k, block, source):
        rows = span_of(k)
        return remote(
            part.at[j, rows], rs.at[source, rows], rs_send.at[k, j], rs_recv.at[k, source], place(block)
        )

    def part_block_last(j):
        return c * n + j

    def part_block(j):
        return jnp.where(c == 0, j * nb + v, v * nb + j) * ntp + c

    def dense(k, count, block_of, source, start, weight, grad):
        rows = span_of(k)

        def one(step, carry):
            j = lax.rem(step + start, count)
            block = block_of(j)
            copy = part_copy(j, k, block, source)
            w_rows = pl.ds(pl.multiple_of(j * cb + k * chunk, chunk), chunk)
            product = jnp.dot(
                weight[w_rows, :], grad[...], preferred_element_type=F32
            ).astype(BF16)

            @pl.when(block != b)
            def _():
                part[j, rows, :] = product
                copy.start()

            @pl.when(block == b)
            def _():
                rs[source, rows, :] = product

            return carry

        lax.fori_loop(0, count, one, 0)

    @pl.when(last)
    def _():
        for source in range(n):

            @pl.when(jnp.logical_or(source != q, jnp.logical_not(owns)))
            def _():
                remote(
                    og_hbm.at[:, pl.ds(0, cb)],
                    gin.at[pl.ds(source * tl, tl)],
                    og_send.at[0],
                    og_recv.at[source],
                    sibling,
                ).wait_recv()

        for k in range(chunks):
            gbuf[grad_rows(v, c, k), :] = (
                gin[:, pl.ds(k * chunk, chunk)].astype(F32).T.astype(BF16)
            )
            sib_copy(k).start()
        w_copy.wait()
        for k in range(chunks):
            gather_wait(k, v, 1 - c)

        def all_dense(k, carry):
            dense(k, n, part_block_last, q, slot + 1, w_vmem, gbuf.at[aligned(v, chip)])
            return carry

        lax.fori_loop(0, chunks, all_dense, 0)

    x_local.wait()
    for r in range(1, m):
        source = lax.rem(b - r + m, m)
        remote(
            x_hbm.at[:, pl.ds(0, cb)],
            xin.at[aligned(source, x_rows)],
            x_send.at[r],
            x_recv.at[r],
            sibling,
        ).wait_recv()
    for k in range(chunks):
        span = pl.ds(k * chunk, chunk)
        xt[span, :] = xin[:, span].astype(F32).T

    @pl.when(jnp.logical_not(owns))
    def _():
        taps_copy.wait_recv()
        filt_copy.wait_recv()

    cols[...] = taps_in[...].T
    lane = lax.broadcasted_iota(jnp.int32, (gw, tokens), 1)

    def later(value, by):
        if by == 0:
            return value
        return jnp.where(lane >= by, pltpu.roll(value, by, 1), 0.0)

    def stacked(value):
        return jnp.concatenate(
            [value[:, i * width : (i + 1) * width] for i in range(blocks)], axis=0
        )

    def windows(value):
        wide = jnp.concatenate([value, jnp.zeros((gw, width), value.dtype)], axis=1)
        return jnp.concatenate(
            [wide[:, i * width : (i + 2) * width] for i in range(blocks)], axis=0
        )

    def group_rows(g):
        return aligned(g, gw)

    def recompute(g, carry):
        rows = group_rows(g)
        source = xt[rows, :]
        weight = cols[rows, :]
        running = [jnp.zeros((gw, tokens), F32)] * 3
        for j in range(taps):
            shifted = later(source, j)
            for f in range(3):
                running[f] = running[f] + weight[:, 3 * j + f : 3 * j + f + 1] * shifted
        for f in range(3):
            feats[f, rows, :] = running[f]
        product = (running[1] * running[2]).astype(BF16)
        kv[rows, :] = product
        tap_row = jnp.concatenate([filt[pl.ds(g, 1), :], jnp.zeros((1, width), F32)], axis=1)
        band = pltpu.roll(
            jnp.broadcast_to(tap_row, (width, 2 * width)), 0, 1, stride=1, stride_axis=0
        ).astype(BF16)
        toep[g] = band
        spread = jnp.dot(stacked(product), band, preferred_element_type=F32)
        for i in range(blocks):
            value = spread[i * gw : (i + 1) * gw, :width]
            if i > 0:
                value = value + spread[(i - 1) * gw : i * gw, width:]
            mixed[rows, pl.ds(i * width, width)] = value
        return carry

    lax.fori_loop(0, groups, recompute, 0, unroll=2)

    def z_copy(k):
        return remote(
            ig.at[span_of(k)],
            gbuf.at[grad_rows(v, c, k)],
            z_send.at[k],
            z_recv.at[k],
            (jnp.maximum(p - 1, 0), q, c),
        )

    @pl.when(jnp.logical_not(last))
    def _():
        for k in range(chunks):
            z_copy(k).wait_recv()
            for copy in gather_copies(k):
                copy.start()
            sib_copy(k).start()
        swap_arrived()
        for k in range(chunks):
            gather_wait(k, v, 1 - c)
            for r in range(1, nb):
                for core in range(ntp):
                    gather_wait(k, lax.rem(v + r, nb), core)
        dense(0, nb, part_block, u, u + 1, w_swap, gbuf)

    per_chunk = chunk // gw
    batch = 2 if per_chunk % 2 == 0 else 1
    bulk = batch * gw
    bulk_lane = lax.broadcasted_iota(jnp.int32, (bulk, tokens), 1)

    def backward(s, carry):
        rows = aligned(s, bulk)
        gate = gate_sum[rows, :].astype(F32)
        mixed_grad = (gate * feats[0, rows, :]).astype(BF16)
        pieces = []
        for r in range(batch):
            result = lax.dot_general(
                windows(mixed_grad[r * gw : (r + 1) * gw]),
                toep[s * batch + r],
                (((1,), (1,)), ((), ())),
                preferred_element_type=F32,
            )
            pieces.append(
                jnp.concatenate([result[i * gw : (i + 1) * gw] for i in range(blocks)], axis=1)
            )
        product_grad = jnp.concatenate(pieces, axis=0)
        query_grad = gate * mixed[rows, :]
        grads = (query_grad, product_grad * feats[2, rows, :], product_grad * feats[1, rows, :])
        weight = cols[rows, :]
        own = pl.ds(pl.multiple_of((v * ntp + c) * cb + s * bulk, bulk), bulk)
        total = gbuf[own, :].astype(F32)
        for j in range(taps):
            term = weight[:, 3 * j : 3 * j + 1] * grads[0]
            for f in (1, 2):
                term = term + weight[:, 3 * j + f : 3 * j + f + 1] * grads[f]
            if j:
                turned = pltpu.roll(term, tokens - j, 1)
                term = jnp.where(bulk_lane < tokens - j, turned, 0.0)
            total = total + term
        dm[rows, :] = mixed_grad
        dkv[rows, :] = product_grad
        mixed[rows, :] = query_grad
        ig[rows, :] = total.astype(BF16)
        return carry

    def chunk_groups(k, body):
        lax.fori_loop(0, per_chunk, lambda i, carry: body(k * per_chunk + i, carry), 0, unroll=2)

    def arrived(k, count, self_source, kept):
        rows = span_of(k)
        for source in range(count):

            @pl.when(jnp.logical_or(source != self_source, jnp.logical_not(kept)))
            def _():
                remote(
                    part.at[0, rows],
                    rs.at[source, rows],
                    rs_send.at[k, 0],
                    rs_recv.at[k, source],
                    sibling,
                ).wait_recv()

        def add(g, carry):
            part_rows = group_rows(g)
            total = rs[0, part_rows, :].astype(F32)
            for source in range(1, count):
                total = total + rs[source, part_rows, :].astype(F32)
            gate_sum[part_rows, :] = total.astype(BF16)
            return carry

        chunk_groups(k, add)

    def give(src, dst, send_sem, recv_sem, target):
        copy = remote(src, dst, send_sem, recv_sem, (p, target, half))
        own = pltpu.make_async_copy(src, dst, send_sem)
        away = jnp.logical_or(target != q, jnp.logical_not(owns))

        def start():
            pl.when(away)(copy.start)
            pl.when(jnp.logical_not(away))(own.start)

        def sent():
            pl.when(away)(copy.wait_send)
            pl.when(jnp.logical_not(away))(own.wait)

        return start, sent

    def ig_give(target, k):
        columns = pl.ds(pl.multiple_of(slot * cb + k * chunk, chunk), chunk)
        return give(
            ot.at[pl.ds(target * tl, tl), span_of(k)],
            ig_out.at[:, columns],
            ig_send.at[k, target],
            ig_recv.at[k, slot],
            target,
        )

    def short_give(target):
        return give(
            short_rows,
            short_out.at[:, aligned(slot, cb)],
            sg_send.at[target],
            sg_recv.at[slot],
            target,
        )

    def long_give(target):
        return give(
            long_rows,
            long_out.at[aligned(slot, groups)],
            lg_send.at[target],
            lg_recv.at[slot],
            target,
        )

    def out_chunk(k):
        span = span_of(k)
        ot[:, span] = ig[span, :].astype(F32).T.astype(BF16)
        for target in range(n):
            ig_give(target, k)[0]()

    column = lax.broadcasted_iota(jnp.int32, (gw, TAP_ROWS), 1)
    low = lax.broadcasted_iota(jnp.int32, (8, 2 * width), 0)

    def filters(g, carry):
        rows = group_rows(g)
        source = xt[rows, :]
        product_grad = dkv[rows, :]
        grads = (
            mixed[rows, :],
            product_grad * feats[2, rows, :],
            product_grad * feats[1, rows, :],
        )
        sums = jnp.zeros((gw, TAP_ROWS), F32)
        for j in range(taps):
            shifted = later(source, j)
            for f in range(3):
                total = jnp.sum(grads[f] * shifted, axis=1, keepdims=True)
                sums = jnp.where(column == 3 * j + f, total, sums)
        short_cols[rows, :] = sums
        lags = lax.dot_general(
            stacked(kv[rows, :]),
            windows(dm[rows, :]),
            (((0,), (0,)), ((), ())),
            preferred_element_type=F32,
        )
        size = width
        while size > 8:
            size //= 2
            lags = lags[:size] + pltpu.roll(lags[size:], 2 * width - size, 1)
        for bit in (4, 2, 1):
            lags = jnp.where((low & bit) != 0, pltpu.roll(lags, 2 * width - bit, 1), lags)
        long_rows[pl.ds(g, 1), :] = jnp.sum(lags, axis=0, keepdims=True)[:, :width]
        return carry

    def section_step(k, carry):
        @pl.when(last)
        def _():
            arrived(k, n, q, owns)

        @pl.when(jnp.logical_not(last))
        def _():
            @pl.when(k + 1 < chunks)
            def _():
                dense(k + 1, nb, part_block, u, u + 1, w_swap, gbuf)

            arrived(k, nb, u, True)

        steps = per_chunk // batch
        lax.fori_loop(k * steps, (k + 1) * steps, backward, 0)

        @pl.when(p > 0)
        def _():
            z_copy(k).start()

        @pl.when(p == 0)
        def _():
            out_chunk(k)
            chunk_groups(k, filters)

        return carry

    lax.fori_loop(0, chunks, section_step, 0)

    @pl.when(p > 0)
    def _():
        def finish(k, carry):
            out_chunk(k)
            chunk_groups(k, filters)
            return carry

        lax.fori_loop(0, chunks, finish, 0)

    short_rows[...] = short_cols[...].T
    for target in range(n):
        short_give(target)[0]()
        long_give(target)[0]()

    for j in range(n):

        @pl.when(c * n + j != b)
        def _():
            for k in range(chunks):
                remote(
                    ot.at[pl.ds(0, tl), pl.ds(0, chunk)],
                    ig_out.at[:, pl.ds(j * cb + k * chunk, chunk)],
                    ig_send.at[k, 0],
                    ig_recv.at[k, j],
                    sibling,
                ).wait_recv()
            for src, dst, send, recv in (
                (short_rows, short_out.at[:, pl.ds(j * cb, cb)], sg_send, sg_recv),
                (long_rows, long_out.at[pl.ds(j * groups, groups)], lg_send, lg_recv),
            ):
                remote(src, dst, send.at[0], recv.at[j], sibling).wait_recv()

    for target in range(n):
        short_give(target)[1]()
        long_give(target)[1]()
        for k in range(chunks):
            ig_give(target, k)[1]()
    for r in range(1, m):
        x_copy(r).wait_send()

    @pl.when(owns)
    def _():
        taps_copy.wait_send()
        filt_copy.wait_send()

    @pl.when(last)
    def _():
        for j in range(n):
            block, copy = og_copy(j)

            @pl.when(block != b)
            def _():
                copy.wait_send()
                for k in range(chunks):
                    part_copy(j, k, block, q).wait_send()

    @pl.when(jnp.logical_not(last))
    def _():
        for j in range(nb):
            block = part_block(j)

            @pl.when(block != b)
            def _():
                for k in range(chunks):
                    part_copy(j, k, block, u).wait_send()

        swap_sent()
        for k in range(chunks):
            for copy in gather_copies(k):
                copy.wait_send()

    for k in range(chunks):
        sib_copy(k).wait_send()

        @pl.when(p > 0)
        def _():
            z_copy(k).wait_send()


def per_device(layer_inputs, out_grad, short_weights, long_filters, out_weights):
    sections, n, ntp = (lax.axis_size(a) for a in ("pipe", "seq", "tp"))
    m = n * ntp
    channels = layer_inputs.shape[2]
    tokens = layer_inputs.shape[1] * m
    cb = channels // m
    taps = short_weights.shape[1]
    width = long_filters.shape[2]
    groups = long_filters.shape[1] // n
    half = channels // ntp
    chunk = min(128, cb)
    chunks = cb // chunk
    nb = max(d for d in range(1, n + 1) if d * d <= n)
    assert nb * nb == n and nb % ntp == 0
    halves = nb // ntp
    dims = (sections, n, nb, ntp, tokens, cb, groups, width, taps, chunk)
    tap_rows = jnp.pad(
        short_weights.reshape(taps * 3, half).astype(F32), ((0, TAP_ROWS - taps * 3), (0, 0))
    )
    dma = pltpu.SemaphoreType.DMA
    anywhere = pl.BlockSpec(memory_space=pl.ANY)
    input_grad, short_grad, long_grad = pl.pallas_call(
        functools.partial(kernel, dims),
        out_shape=(
            jax.ShapeDtypeStruct((tokens // n, half), BF16),
            jax.ShapeDtypeStruct((TAP_ROWS, half), F32),
            jax.ShapeDtypeStruct((groups * n, width), F32),
        ),
        in_specs=[anywhere] * 5,
        out_specs=(anywhere,) * 3,
        scratch_shapes=[
            pltpu.VMEM((tokens, cb), BF16),
            pltpu.VMEM((tokens, cb), BF16),
            pltpu.VMEM((TAP_ROWS, cb), F32),
            pltpu.VMEM((groups, width), F32),
            pltpu.VMEM((half, channels // n), BF16),
            pltpu.VMEM((nb * cb, channels // nb), BF16),
            pltpu.VMEM((cb, tokens), BF16),
            pltpu.VMEM((cb, tokens), F32),
            pltpu.VMEM((cb, TAP_ROWS), F32),
            pltpu.VMEM((3, cb, tokens), F32),
            pltpu.VMEM((cb, tokens), F32),
            pltpu.VMEM((cb, tokens), F32),
            pltpu.VMEM((cb, tokens), BF16),
            pltpu.VMEM((cb, tokens), BF16),
            pltpu.VMEM((groups, width, 2 * width), BF16),
            pltpu.VMEM((nb * ntp * cb, tokens), BF16),
            pltpu.VMEM((n, cb, tokens), BF16),
            pltpu.VMEM((n, cb, tokens), BF16),
            pltpu.VMEM((cb, tokens), BF16),
            pltpu.VMEM((tokens, cb), BF16),
            pltpu.VMEM((cb, TAP_ROWS), F32),
            pltpu.VMEM((TAP_ROWS, cb), F32),
            pltpu.VMEM((groups, width), F32),
            dma((m,)),
            dma((m,)),
            dma((n,)),
            dma((n,)),
            dma((2,)),
            dma((2,)),
            dma((chunks, 2 * nb - 1)),
            dma((chunks, nb * ntp)),
            dma((ntp, nb * halves)),
            dma((n,)),
            dma((chunks,)),
            dma((chunks,)),
            dma((chunks, n)),
            dma((chunks, n)),
            dma((chunks, n)),
            dma((chunks, n)),
            dma((n,)),
            dma((n,)),
            dma((n,)),
            dma((n,)),
            dma((8,)),
        ],
        compiler_params=pltpu.CompilerParams(
            collective_id=0, has_side_effects=True, vmem_limit_bytes=52 * 1024 * 1024
        ),
        name="sections_backward",
    )(layer_inputs[0], out_grad, tap_rows, long_filters[0].astype(F32), out_weights[0])
    short_result = short_grad[: taps * 3].reshape(1, taps, 3, half)
    return (input_grad[None], short_result, long_grad[None])


def solution(mesh):
    in_specs = (
        P("pipe", ("seq", "tp"), None),
        P("seq", "tp"),
        P("pipe", None, None, "tp"),
        P("pipe", "tp", None),
        P("pipe", "tp", "seq"),
    )
    out_specs = (P("pipe", "seq", "tp"), P("pipe", None, None, "tp"), P("pipe", "tp", None))
    return jax.shard_map(
        per_device, mesh=mesh, in_specs=in_specs, out_specs=out_specs, check_vma=False
    )
```

```python
import functools

import jax
import jax.numpy as jnp
from jax import lax
from jax.experimental import pallas as pl
from jax.experimental.pallas import tpu as pltpu
from jax.sharding import PartitionSpec as P

MESH = pl.DeviceIdType.MESH
F32 = jnp.float32
BF16 = jnp.bfloat16
TAP_ROWS = 32


def remote(src, dst, send_sem, recv_sem, device):
    return pltpu.make_async_remote_copy(
        src_ref=src,
        dst_ref=dst,
        send_sem=send_sem,
        recv_sem=recv_sem,
        device_id=device,
        device_id_type=MESH,
    )


def aligned(index, size):
    return pl.ds(pl.multiple_of(index * size, size), size)


def kernel(
    dims,
    x_hbm,
    og_hbm,
    taps_hbm,
    filt_hbm,
    w_hbm,
    ig_out,
    short_out,
    long_out,
    xin,
    gin,
    taps_in,
    filt,
    w_vmem,
    w_swap,
    gate_sum,
    xt,
    cols,
    feats,
    mixed,
    dkv,
    kv,
    dm,
    toep,
    gbuf,
    part,
    rs,
    ig,
    ot,
    short_cols,
    short_rows,
    long_rows,
    x_send,
    x_recv,
    og_send,
    og_recv,
    small_send,
    small_recv,
    ag_send,
    ag_recv,
    ws_send,
    ws_recv,
    z_send,
    z_recv,
    rs_send,
    rs_recv,
    ig_send,
    ig_recv,
    sg_send,
    sg_recv,
    lg_send,
    lg_recv,
    local_sem,
):
    sections, n, nb, ntp, tokens, cb, groups, width, taps, chunk = dims
    halves = nb // ntp
    chip = ntp * cb
    m = n * ntp
    chunks = cb // chunk
    blocks = tokens // width
    gw = cb // groups
    tl = tokens // n
    p, q, c = lax.axis_index("pipe"), lax.axis_index("seq"), lax.axis_index("tp")
    b = q * ntp + c
    half, slot = b // n, lax.rem(b, n)
    a, e = q // nb, lax.rem(q, nb)
    u, v = jnp.where(c == 0, a, e), jnp.where(c == 0, e, a)
    sibling = (p, q, 1 - c)
    owns = c == half
    last = p == sections - 1

    def place(block):
        return (p, block // ntp, lax.rem(block, ntp))

    barrier = pltpu.get_barrier_semaphore()
    for r in range(1, m):
        pl.semaphore_signal(
            barrier, inc=1, device_id=place(lax.rem(b + r, m)), device_id_type=MESH
        )

    @pl.when(p > 0)
    def _():
        pl.semaphore_signal(barrier, inc=1, device_id=(p - 1, q, c), device_id_type=MESH)

    @pl.when(p < sections - 1)
    def _():
        pl.semaphore_signal(barrier, inc=1, device_id=(p + 1, q, c), device_id_type=MESH)

    w_copy = pltpu.make_async_copy(w_hbm, w_vmem, local_sem.at[0])

    @pl.when(last)
    def _():
        w_copy.start()

    def swap_pieces():
        for i in range(halves):
            for j in range(nb):
                to, row = j, c * halves + i
                yield 0, i * nb + j, a * nb + to, row, row * nb + to, e
                to, row = c * halves + i, j
                yield 1, i * nb + j, to * nb + e, row, to * nb + row, a

    def swap_copies(piece):
        core, index, chip_to, row, owner, column = piece
        local = owner - c * (n // ntp)
        src = w_hbm.at[pl.ds(pl.multiple_of(local * chip + core * cb, cb), cb)]
        dst = w_swap.at[aligned(row, cb), aligned(column, chip)]
        send = ws_send.at[core, index]
        far = remote(src, dst, send, ws_recv.at[row * nb + column], (p, chip_to, core))
        near = pltpu.make_async_copy(src, dst, send)
        return jnp.logical_or(chip_to != q, core != c), far, near

    def swap_start():
        for piece in swap_pieces():
            away, far, near = swap_copies(piece)
            pl.when(away)(far.start)
            pl.when(jnp.logical_not(away))(near.start)

    def swap_sent():
        for piece in swap_pieces():
            away, far, near = swap_copies(piece)
            pl.when(away)(far.wait_send)

    def swap_arrived():
        for piece in swap_pieces():
            away, far, near = swap_copies(piece)
            pl.when(jnp.logical_not(away))(near.wait)
        for row in range(nb):
            owner = jnp.where(c == 0, row * nb + v, v * nb + row)
            for column in range(nb):
                away = jnp.logical_or(column != v, owner // (n // ntp) != c)
                far = remote(
                    w_hbm.at[pl.ds(0, cb)],
                    w_swap.at[pl.ds(row * cb, cb), pl.ds(column * chip, chip)],
                    ws_send.at[0, 0],
                    ws_recv.at[row * nb + column],
                    sibling,
                )
                pl.when(away)(far.wait_recv)

    x_rows = tokens // m
    x_local = pltpu.make_async_copy(
        x_hbm.at[:, aligned(b, cb)], xin.at[aligned(b, x_rows)], local_sem.at[1]
    )
    x_local.start()
    ends = (p > 0).astype(jnp.int32) + (p < sections - 1).astype(jnp.int32)
    pl.semaphore_wait(barrier, m - 1 + ends)

    def og_copy(j):
        block = c * n + j
        return block, remote(
            og_hbm.at[:, aligned(j, cb)],
            gin.at[aligned(q, tl)],
            og_send.at[j],
            og_recv.at[q],
            place(block),
        )

    @pl.when(last)
    def _():
        for j in range(n):
            block, copy = og_copy(j)

            @pl.when(block != b)
            def _():
                copy.start()

        @pl.when(owns)
        def _():
            own = pltpu.make_async_copy(
                og_hbm.at[:, aligned(slot, cb)], gin.at[aligned(q, tl)], local_sem.at[2]
            )
            own.start()
            own.wait()

    def x_copy(r):
        block = lax.rem(b + r, m)
        return remote(
            x_hbm.at[:, aligned(block, cb)],
            xin.at[aligned(b, x_rows)],
            x_send.at[r],
            x_recv.at[r],
            place(block),
        )

    for r in range(1, m):
        x_copy(r).start()

    other = lax.rem(q * ntp + 1 - c, n)
    taps_copy = remote(
        taps_hbm.at[:, aligned(other, cb)], taps_in, small_send.at[0], small_recv.at[0], sibling
    )
    filt_copy = remote(
        filt_hbm.at[aligned(other, groups)], filt, small_send.at[1], small_recv.at[1], sibling
    )

    @pl.when(owns)
    def _():
        taps_copy.start()
        filt_copy.start()
        taps_own = pltpu.make_async_copy(
            taps_hbm.at[:, aligned(slot, cb)], taps_in, local_sem.at[3]
        )
        filt_own = pltpu.make_async_copy(filt_hbm.at[aligned(slot, groups)], filt, local_sem.at[4])
        taps_own.start()
        filt_own.start()
        taps_own.wait()
        filt_own.wait()

    pl.when(jnp.logical_not(last))(swap_start)

    def grad_rows(at, core, k):
        return pl.ds(pl.multiple_of((at * ntp + core) * cb + k * chunk, chunk), chunk)

    def gather_copy(k, index, at, device):
        return remote(
            gbuf.at[grad_rows(v, c, k)],
            gbuf.at[grad_rows(at, c, k)],
            ag_send.at[k, index],
            ag_recv.at[k, at * ntp + c],
            device,
        )

    def sib_copy(k):
        return gather_copy(k, 0, u, sibling)

    def gather_copies(k):
        copies = []
        for r in range(1, nb):
            to = lax.rem(e + r, nb)
            copies.append(gather_copy(k, r, e, (p, a * nb + to, 0)))
            to = lax.rem(a + r, nb)
            copies.append(gather_copy(k, nb - 1 + r, a, (p, to * nb + e, 1)))
        return copies

    def gather_wait(k, at, core):
        ref = gbuf.at[grad_rows(at, core, k)]
        remote(ref, ref, ag_send.at[k, 0], ag_recv.at[k, at * ntp + core], sibling).wait_recv()

    def span_of(k):
        return pl.ds(pl.multiple_of(k * chunk, chunk), chunk)

    def part_copy(j, k, block, source):
        rows = span_of(k)
        return remote(
            part.at[j, rows], rs.at[source, rows], rs_send.at[k, j], rs_recv.at[k, source], place(block)
        )

    def part_block_last(j):
        return c * n + j

    def part_block(j):
        return jnp.where(c == 0, j * nb + v, v * nb + j) * ntp + c

    def dense(k, count, block_of, source, start, weight, grad):
        rows = span_of(k)

        def one(step, carry):
            pair = [lax.rem(2 * step + i + start, count) for i in range(2)]
            taken = [weight[pl.ds(pl.multiple_of(j * cb + k * chunk, chunk), chunk), :] for j in pair]
            both = jnp.dot(
                jnp.concatenate(taken, axis=0), grad[...], preferred_element_type=F32
            ).astype(BF16)
            for i, j in enumerate(pair):
                block = block_of(j)
                copy = part_copy(j, k, block, source)
                product = both[i * chunk : (i + 1) * chunk]

                @pl.when(block != b)
                def _():
                    part[j, rows, :] = product
                    copy.start()

                @pl.when(block == b)
                def _():
                    rs[source, rows, :] = product

            return carry

        lax.fori_loop(0, count // 2, one, 0)

    @pl.when(last)
    def _():
        for source in range(n):

            @pl.when(jnp.logical_or(source != q, jnp.logical_not(owns)))
            def _():
                remote(
                    og_hbm.at[:, pl.ds(0, cb)],
                    gin.at[pl.ds(source * tl, tl)],
                    og_send.at[0],
                    og_recv.at[source],
                    sibling,
                ).wait_recv()

        for k in range(chunks):
            gbuf[grad_rows(v, c, k), :] = (
                gin[:, pl.ds(k * chunk, chunk)].astype(F32).T.astype(BF16)
            )
            sib_copy(k).start()
        w_copy.wait()
        for k in range(chunks):
            gather_wait(k, v, 1 - c)

        def all_dense(k, carry):
            dense(k, n, part_block_last, q, slot + 1, w_vmem, gbuf.at[aligned(v, chip)])
            return carry

        lax.fori_loop(0, chunks, all_dense, 0)

    x_local.wait()
    for r in range(1, m):
        source = lax.rem(b - r + m, m)
        remote(
            x_hbm.at[:, pl.ds(0, cb)],
            xin.at[aligned(source, x_rows)],
            x_send.at[r],
            x_recv.at[r],
            sibling,
        ).wait_recv()
    for k in range(chunks):
        span = pl.ds(k * chunk, chunk)
        xt[span, :] = xin[:, span].astype(F32).T

    @pl.when(jnp.logical_not(owns))
    def _():
        taps_copy.wait_recv()
        filt_copy.wait_recv()

    cols[...] = taps_in[...].T
    lane = lax.broadcasted_iota(jnp.int32, (gw, tokens), 1)

    def later(value, by):
        if by == 0:
            return value
        return jnp.where(lane >= by, pltpu.roll(value, by, 1), 0.0)

    def stacked(value):
        return jnp.concatenate(
            [value[:, i * width : (i + 1) * width] for i in range(blocks)], axis=0
        )

    def windows(value):
        wide = jnp.concatenate([value, jnp.zeros((gw, width), value.dtype)], axis=1)
        return jnp.concatenate(
            [wide[:, i * width : (i + 2) * width] for i in range(blocks)], axis=0
        )

    def group_rows(g):
        return aligned(g, gw)

    def recompute(g, carry):
        rows = group_rows(g)
        source = xt[rows, :]
        weight = cols[rows, :]
        running = [jnp.zeros((gw, tokens), F32)] * 3
        for j in range(taps):
            shifted = later(source, j)
            for f in range(3):
                running[f] = running[f] + weight[:, 3 * j + f : 3 * j + f + 1] * shifted
        for f in range(3):
            feats[f, rows, :] = running[f]
        product = (running[1] * running[2]).astype(BF16)
        kv[rows, :] = product
        tap_row = jnp.concatenate([filt[pl.ds(g, 1), :], jnp.zeros((1, width), F32)], axis=1)
        band = pltpu.roll(
            jnp.broadcast_to(tap_row, (width, 2 * width)), 0, 1, stride=1, stride_axis=0
        ).astype(BF16)
        toep[g] = band
        spread = jnp.dot(stacked(product), band, preferred_element_type=F32)
        for i in range(blocks):
            value = spread[i * gw : (i + 1) * gw, :width]
            if i > 0:
                value = value + spread[(i - 1) * gw : i * gw, width:]
            mixed[rows, pl.ds(i * width, width)] = value
        return carry

    lax.fori_loop(0, groups, recompute, 0, unroll=2)

    def z_copy(k):
        return remote(
            ig.at[span_of(k)],
            gbuf.at[grad_rows(v, c, k)],
            z_send.at[k],
            z_recv.at[k],
            (jnp.maximum(p - 1, 0), q, c),
        )

    @pl.when(jnp.logical_not(last))
    def _():
        for k in range(chunks):
            z_copy(k).wait_recv()
            for copy in gather_copies(k):
                copy.start()
            sib_copy(k).start()
        swap_arrived()
        for k in range(chunks):
            gather_wait(k, v, 1 - c)
            for r in range(1, nb):
                for core in range(ntp):
                    gather_wait(k, lax.rem(v + r, nb), core)
        dense(0, nb, part_block, u, u + 1, w_swap, gbuf)

    per_chunk = chunk // gw
    batch = 2 if per_chunk % 2 == 0 else 1
    bulk = batch * gw
    bulk_lane = lax.broadcasted_iota(jnp.int32, (bulk, tokens), 1)

    def backward(s, carry):
        rows = aligned(s, bulk)
        gate = gate_sum[rows, :].astype(F32)
        mixed_grad = (gate * feats[0, rows, :]).astype(BF16)
        pieces = []
        for r in range(batch):
            result = lax.dot_general(
                windows(mixed_grad[r * gw : (r + 1) * gw]),
                toep[s * batch + r],
                (((1,), (1,)), ((), ())),
                preferred_element_type=F32,
            )
            pieces.append(
                jnp.concatenate([result[i * gw : (i + 1) * gw] for i in range(blocks)], axis=1)
            )
        product_grad = jnp.concatenate(pieces, axis=0)
        query_grad = gate * mixed[rows, :]
        grads = (query_grad, product_grad * feats[2, rows, :], product_grad * feats[1, rows, :])
        weight = cols[rows, :]
        own = pl.ds(pl.multiple_of((v * ntp + c) * cb + s * bulk, bulk), bulk)
        total = gbuf[own, :].astype(F32)
        for j in range(taps):
            term = weight[:, 3 * j : 3 * j + 1] * grads[0]
            for f in (1, 2):
                term = term + weight[:, 3 * j + f : 3 * j + f + 1] * grads[f]
            if j:
                turned = pltpu.roll(term, tokens - j, 1)
                term = jnp.where(bulk_lane < tokens - j, turned, 0.0)
            total = total + term
        dm[rows, :] = mixed_grad
        dkv[rows, :] = product_grad
        mixed[rows, :] = query_grad
        ig[rows, :] = total.astype(BF16)
        return carry

    def chunk_groups(k, body):
        lax.fori_loop(0, per_chunk, lambda i, carry: body(k * per_chunk + i, carry), 0, unroll=2)

    def arrived(k, count, self_source, kept):
        rows = span_of(k)
        for source in range(count):

            @pl.when(jnp.logical_or(source != self_source, jnp.logical_not(kept)))
            def _():
                remote(
                    part.at[0, rows],
                    rs.at[source, rows],
                    rs_send.at[k, 0],
                    rs_recv.at[k, source],
                    sibling,
                ).wait_recv()

        def add(g, carry):
            part_rows = group_rows(g)
            total = rs[0, part_rows, :].astype(F32)
            for source in range(1, count):
                total = total + rs[source, part_rows, :].astype(F32)
            gate_sum[part_rows, :] = total.astype(BF16)
            return carry

        chunk_groups(k, add)

    def give(src, dst, send_sem, recv_sem, target):
        copy = remote(src, dst, send_sem, recv_sem, (p, target, half))
        own = pltpu.make_async_copy(src, dst, send_sem)
        away = jnp.logical_or(target != q, jnp.logical_not(owns))

        def start():
            pl.when(away)(copy.start)
            pl.when(jnp.logical_not(away))(own.start)

        def sent():
            pl.when(away)(copy.wait_send)
            pl.when(jnp.logical_not(away))(own.wait)

        return start, sent

    def ig_give(target, k):
        columns = pl.ds(pl.multiple_of(slot * cb + k * chunk, chunk), chunk)
        return give(
            ot.at[pl.ds(target * tl, tl), span_of(k)],
            ig_out.at[:, columns],
            ig_send.at[k, target],
            ig_recv.at[k, slot],
            target,
        )

    def short_give(target):
        return give(
            short_rows,
            short_out.at[:, aligned(slot, cb)],
            sg_send.at[target],
            sg_recv.at[slot],
            target,
        )

    def long_give(target):
        return give(
            long_rows,
            long_out.at[aligned(slot, groups)],
            lg_send.at[target],
            lg_recv.at[slot],
            target,
        )

    def out_chunk(k):
        span = span_of(k)
        ot[:, span] = ig[span, :].astype(F32).T.astype(BF16)
        for target in range(n):
            ig_give(target, k)[0]()

    column = lax.broadcasted_iota(jnp.int32, (gw, TAP_ROWS), 1)
    low = lax.broadcasted_iota(jnp.int32, (8, 2 * width), 0)

    def filters(g, carry):
        rows = group_rows(g)
        source = xt[rows, :]
        product_grad = dkv[rows, :]
        grads = (
            mixed[rows, :],
            product_grad * feats[2, rows, :],
            product_grad * feats[1, rows, :],
        )
        sums = jnp.zeros((gw, TAP_ROWS), F32)
        for j in range(taps):
            shifted = later(source, j)
            for f in range(3):
                total = jnp.sum(grads[f] * shifted, axis=1, keepdims=True)
                sums = jnp.where(column == 3 * j + f, total, sums)
        short_cols[rows, :] = sums
        lags = lax.dot_general(
            stacked(kv[rows, :]),
            windows(dm[rows, :]),
            (((0,), (0,)), ((), ())),
            preferred_element_type=F32,
        )
        size = width
        while size > 8:
            size //= 2
            lags = lags[:size] + pltpu.roll(lags[size:], 2 * width - size, 1)
        for bit in (4, 2, 1):
            lags = jnp.where((low & bit) != 0, pltpu.roll(lags, 2 * width - bit, 1), lags)
        long_rows[pl.ds(g, 1), :] = jnp.sum(lags, axis=0, keepdims=True)[:, :width]
        return carry

    def section_step(k, carry):
        @pl.when(last)
        def _():
            arrived(k, n, q, owns)

        @pl.when(jnp.logical_not(last))
        def _():
            @pl.when(k + 1 < chunks)
            def _():
                dense(k + 1, nb, part_block, u, u + 1, w_swap, gbuf)

            arrived(k, nb, u, True)

        steps = per_chunk // batch
        lax.fori_loop(k * steps, (k + 1) * steps, backward, 0)

        @pl.when(p > 0)
        def _():
            z_copy(k).start()

        @pl.when(p == 0)
        def _():
            out_chunk(k)
            chunk_groups(k, filters)

        return carry

    lax.fori_loop(0, chunks, section_step, 0)

    @pl.when(p > 0)
    def _():
        def finish(k, carry):
            out_chunk(k)
            chunk_groups(k, filters)
            return carry

        lax.fori_loop(0, chunks, finish, 0)

    short_rows[...] = short_cols[...].T
    for target in range(n):
        short_give(target)[0]()
        long_give(target)[0]()

    for j in range(n):

        @pl.when(c * n + j != b)
        def _():
            for k in range(chunks):
                remote(
                    ot.at[pl.ds(0, tl), pl.ds(0, chunk)],
                    ig_out.at[:, pl.ds(j * cb + k * chunk, chunk)],
                    ig_send.at[k, 0],
                    ig_recv.at[k, j],
                    sibling,
                ).wait_recv()
            for src, dst, send, recv in (
                (short_rows, short_out.at[:, pl.ds(j * cb, cb)], sg_send, sg_recv),
                (long_rows, long_out.at[pl.ds(j * groups, groups)], lg_send, lg_recv),
            ):
                remote(src, dst, send.at[0], recv.at[j], sibling).wait_recv()

    for target in range(n):
        short_give(target)[1]()
        long_give(target)[1]()
        for k in range(chunks):
            ig_give(target, k)[1]()
    for r in range(1, m):
        x_copy(r).wait_send()

    @pl.when(owns)
    def _():
        taps_copy.wait_send()
        filt_copy.wait_send()

    @pl.when(last)
    def _():
        for j in range(n):
            block, copy = og_copy(j)

            @pl.when(block != b)
            def _():
                copy.wait_send()
                for k in range(chunks):
                    part_copy(j, k, block, q).wait_send()

    @pl.when(jnp.logical_not(last))
    def _():
        for j in range(nb):
            block = part_block(j)

            @pl.when(block != b)
            def _():
                for k in range(chunks):
                    part_copy(j, k, block, u).wait_send()

        swap_sent()
        for k in range(chunks):
            for copy in gather_copies(k):
                copy.wait_send()

    for k in range(chunks):
        sib_copy(k).wait_send()

        @pl.when(p > 0)
        def _():
            z_copy(k).wait_send()


def per_device(layer_inputs, out_grad, short_weights, long_filters, out_weights):
    sections, n, ntp = (lax.axis_size(a) for a in ("pipe", "seq", "tp"))
    m = n * ntp
    channels = layer_inputs.shape[2]
    tokens = layer_inputs.shape[1] * m
    cb = channels // m
    taps = short_weights.shape[1]
    width = long_filters.shape[2]
    groups = long_filters.shape[1] // n
    half = channels // ntp
    chunk = min(128, cb)
    chunks = cb // chunk
    nb = max(d for d in range(1, n + 1) if d * d <= n)
    assert nb * nb == n and nb % ntp == 0
    halves = nb // ntp
    dims = (sections, n, nb, ntp, tokens, cb, groups, width, taps, chunk)
    tap_rows = jnp.pad(
        short_weights.reshape(taps * 3, half).astype(F32), ((0, TAP_ROWS - taps * 3), (0, 0))
    )
    dma = pltpu.SemaphoreType.DMA
    anywhere = pl.BlockSpec(memory_space=pl.ANY)
    input_grad, short_grad, long_grad = pl.pallas_call(
        functools.partial(kernel, dims),
        out_shape=(
            jax.ShapeDtypeStruct((tokens // n, half), BF16),
            jax.ShapeDtypeStruct((TAP_ROWS, half), F32),
            jax.ShapeDtypeStruct((groups * n, width), F32),
        ),
        in_specs=[anywhere] * 5,
        out_specs=(anywhere,) * 3,
        scratch_shapes=[
            pltpu.VMEM((tokens, cb), BF16),
            pltpu.VMEM((tokens, cb), BF16),
            pltpu.VMEM((TAP_ROWS, cb), F32),
            pltpu.VMEM((groups, width), F32),
            pltpu.VMEM((half, channels // n), BF16),
            pltpu.VMEM((nb * cb, channels // nb), BF16),
            pltpu.VMEM((cb, tokens), BF16),
            pltpu.VMEM((cb, tokens), F32),
            pltpu.VMEM((cb, TAP_ROWS), F32),
            pltpu.VMEM((3, cb, tokens), F32),
            pltpu.VMEM((cb, tokens), F32),
            pltpu.VMEM((cb, tokens), F32),
            pltpu.VMEM((cb, tokens), BF16),
            pltpu.VMEM((cb, tokens), BF16),
            pltpu.VMEM((groups, width, 2 * width), BF16),
            pltpu.VMEM((nb * ntp * cb, tokens), BF16),
            pltpu.VMEM((n, cb, tokens), BF16),
            pltpu.VMEM((n, cb, tokens), BF16),
            pltpu.VMEM((cb, tokens), BF16),
            pltpu.VMEM((tokens, cb), BF16),
            pltpu.VMEM((cb, TAP_ROWS), F32),
            pltpu.VMEM((TAP_ROWS, cb), F32),
            pltpu.VMEM((groups, width), F32),
            dma((m,)),
            dma((m,)),
            dma((n,)),
            dma((n,)),
            dma((2,)),
            dma((2,)),
            dma((chunks, 2 * nb - 1)),
            dma((chunks, nb * ntp)),
            dma((ntp, nb * halves)),
            dma((n,)),
            dma((chunks,)),
            dma((chunks,)),
            dma((chunks, n)),
            dma((chunks, n)),
            dma((chunks, n)),
            dma((chunks, n)),
            dma((n,)),
            dma((n,)),
            dma((n,)),
            dma((n,)),
            dma((8,)),
        ],
        compiler_params=pltpu.CompilerParams(
            collective_id=0, has_side_effects=True, vmem_limit_bytes=52 * 1024 * 1024
        ),
        name="sections_backward",
    )(layer_inputs[0], out_grad, tap_rows, long_filters[0].astype(F32), out_weights[0])
    short_result = short_grad[: taps * 3].reshape(1, taps, 3, half)
    return (input_grad[None], short_result, long_grad[None])


def solution(mesh):
    in_specs = (
        P("pipe", ("seq", "tp"), None),
        P("seq", "tp"),
        P("pipe", None, None, "tp"),
        P("pipe", "tp", None),
        P("pipe", "tp", "seq"),
    )
    out_specs = (P("pipe", "seq", "tp"), P("pipe", None, None, "tp"), P("pipe", "tp", None))
    return jax.shard_map(
        per_device, mesh=mesh, in_specs=in_specs, out_specs=out_specs, check_vma=False
    )
```
